32 devices in a mesh: groups: 2 (over y), ctx: 4 (over z), heads: 4 (over x, core).
Axes of the slice: x: 2, y: 2, z: 4, core: 2. Of those that a mesh axis runs over, the one named last changes fastest.
Arguments:
- queries: bfloat16 [4096, 28, 128], P(('groups', 'ctx'), 'heads'), parts along dimension 0, may hold values from -9 to 9
- key_states: bfloat16 [4096, 4, 128], P(('groups', 'ctx'), 'heads'), parts along dimension 0, may hold values from -9 to 9
- value_states: bfloat16 [4096, 4, 128], P(('groups', 'ctx'), 'heads'), parts along dimension 0, may hold values from -6 to 6
- out_weight: bfloat16 [3584, 3584], P('heads'), may hold values from -1.5 to 1.5
- slash_offsets: int32 [8, 8], P(('groups', 'heads')), parts along dimension 0, may hold values from 0 to 23, as said below
- vertical_blocks: int32 [8, 4], P(('groups', 'heads')), parts along dimension 0, may hold values from 0 to 7
Outputs:
- output: bfloat16 [4096, 3584], P(('groups', 'ctx'), 'heads'), parts along dimension 0
The draws below stay inside these ranges and needn't reach their ends.
There are 2 independent parts, one for each index of `groups`. The reference program is written for one: setup_inputs(seed, part) draws one part's arguments, and reference() takes and returns one part's arrays. A program takes and returns all parts, laid end to end along the dimension named above; an argument that names none is the same for every part. Nothing has to cross between parts.
Inputs may be any that keep to these rules, and one draw needn't show every extreme that they name: `slash_offsets`: each key-value head's 8 offsets are distinct and include 0 and 3 * 512 // 64 - 1.
All inputs are finite; a program needn't handle non-finite values.
Results may differ from the reference program's by a relative error of at most 0.011.
Values may be sent and summed in bfloat16 or wider, within the bound.
No kernel may reach another device: no remote copies, remote signals or barrier semaphores. Data moves between devices by JAX's collectives and lax.ppermute only.
A program may use at most 192 MiB of HBM per device.

```python
import jax
import jax.numpy as jnp
from jax import lax

D = 3584
Q_HEADS = 28
KV_HEADS = 4
HEAD = 128
TOK_DEV = 512
BLOCK = 64
BAND = 3
SLASH = 8
SEQ = 2048
N_CTX = 4


def draw_queries(key, part):
    key = jax.random.fold_in(key, 11)
    result = 1.2 * jax.random.normal(key, (SEQ, Q_HEADS, HEAD), jnp.float32)
    return jnp.clip(result, -9.0, 9.0).astype(jnp.bfloat16)


def draw_key_states(key, part):
    key = jax.random.fold_in(key, 12)
    result = 1.2 * jax.random.normal(key, (SEQ, KV_HEADS, HEAD), jnp.float32)
    return jnp.clip(result, -9.0, 9.0).astype(jnp.bfloat16)


def shuffled_offsets(sub_key):
    band_span = BAND * TOK_DEV // BLOCK
    return jax.random.permutation(sub_key, band_span - 2) + 1


def draw_slash_offsets(key, part):
    key = jax.random.fold_in(key, 13)
    band_span = BAND * TOK_DEV // BLOCK
    head_keys = jax.random.split(key, KV_HEADS)
    picked = jax.vmap(shuffled_offsets)(head_keys)[:, :SLASH - 2].astype(jnp.int32)
    first_col = jnp.zeros((KV_HEADS, 1), jnp.int32)
    last_col = jnp.full((KV_HEADS, 1), band_span - 1, jnp.int32)
    return jnp.concatenate([first_col, last_col, picked], axis=1)


def with_ends(array, own_key, low, high):
    index_at = [jax.random.randint(jax.random.fold_in(own_key, axis), (), 0, length) for axis, length in enumerate(array.shape)]
    main_axis = array.shape.index(max(array.shape))
    next_to = index_at[:main_axis] + [(index_at[main_axis] + 1) % array.shape[main_axis]] + index_at[main_axis + 1:]
    return array.at[tuple(index_at)].set(low).at[tuple(next_to)].set(high)


def block_levels(own_key, shape, cuts, least, high):
    def one(axis_at, blocks):
        steps = jax.random.uniform(jax.random.fold_in(jax.random.fold_in(own_key, 6), axis_at), (blocks,), jnp.float32, least / len(cuts), high / len(cuts))
        return jnp.repeat(jnp.exp(steps), shape[axis_at] // blocks).reshape((-1,) + (1,) * (len(shape) - axis_at - 1))

    gain = one(*cuts[0])
    for cut in cuts[1:]:
        gain = gain * one(*cut)
    return gain


def normal_values(stream_key, dims, scale, limit, cuts=(), held_as=jnp.bfloat16):
    values = scale * jax.random.normal(stream_key, dims, jnp.float32)
    if cuts:
        values = values * block_levels(stream_key, dims, cuts, -0.22, 0.18)
    return jnp.clip(values, -limit, limit).astype(held_as)


def setup_inputs(seed: int = 0, part: int = 0) -> dict:
    arg_keys = jax.random.split(jax.random.key(seed), 7)
    own_keys = jax.random.split(jax.random.fold_in(arg_keys[6], part), 7)
    return {
        "queries": draw_queries(jax.random.fold_in(jax.random.fold_in(arg_keys[6], part), 71), part),
        "key_states": draw_key_states(jax.random.fold_in(jax.random.fold_in(arg_keys[6], part), 71), part),
        "value_states": normal_values(own_keys[2], (SEQ, KV_HEADS, HEAD), 1.0, 6.0, ((0, 4), (1, 4))),
        "out_weight": normal_values(arg_keys[3], (Q_HEADS * HEAD, D), (HEAD // 8) ** -0.5, 1.5, ((0, 4),)),
        "slash_offsets": draw_slash_offsets(jax.random.fold_in(jax.random.fold_in(arg_keys[6], part), 71), part),
        "vertical_blocks": with_ends(jax.random.randint(own_keys[5], (KV_HEADS, N_CTX), 0, TOK_DEV // BLOCK), jax.random.fold_in(own_keys[5], 1), 0, (TOK_DEV // BLOCK) - 1).astype(jnp.int32),
    }


def band_member(distance, offsets):
    return jnp.any(distance[..., None] == offsets, axis=-1)


def reference(queries, key_states, value_states, out_weight, slash_offsets, vertical_blocks):
    per_group = Q_HEADS // KV_HEADS
    blocks = TOK_DEV // BLOCK
    score_scale = HEAD ** -0.5
    leading = jnp.zeros((BAND * TOK_DEV, KV_HEADS, HEAD), key_states.dtype)
    padded_keys = jnp.concatenate([leading, key_states], axis=0)
    padded_values = jnp.concatenate([leading, value_states], axis=0)
    within_tile = jnp.arange(BLOCK, dtype=jnp.int32)

    def shard_output(shard_index):
        query_rows = lax.dynamic_slice_in_dim(queries, shard_index * TOK_DEV, TOK_DEV, 0)
        band_keys = lax.dynamic_slice_in_dim(padded_keys, shard_index * TOK_DEV, (BAND + 1) * TOK_DEV, 0)
        band_values = lax.dynamic_slice_in_dim(padded_values, shard_index * TOK_DEV, (BAND + 1) * TOK_DEV, 0)
        query_pos = shard_index * TOK_DEV + jnp.arange(TOK_DEV, dtype=jnp.int32)
        query_block = query_pos // BLOCK
        window = jnp.arange((BAND + 1) * TOK_DEV, dtype=jnp.int32)
        key_pos = (shard_index - BAND) * TOK_DEV + window
        key_block = key_pos // BLOCK
        partial_sum = jnp.zeros((TOK_DEV, D), jnp.float32)
        for kv_head in range(KV_HEADS):
            offsets = slash_offsets[kv_head]
            vert_block = jnp.arange(N_CTX, dtype=jnp.int32) * blocks + vertical_blocks[kv_head].astype(jnp.int32)
            vert_pos = (vert_block[:, None] * BLOCK + within_tile[None, :]).reshape(-1)
            key_set = jnp.concatenate([band_keys[:, kv_head], key_states[vert_pos, kv_head]], axis=0).astype(jnp.float32)
            value_set = jnp.concatenate([band_values[:, kv_head], value_states[vert_pos, kv_head]], axis=0).astype(jnp.float32)
            band_gap = query_block[:, None] - key_block[None, :]
            band_allowed = band_member(band_gap, offsets) & (key_pos[None, :] <= query_pos[:, None]) & (key_pos[None, :] >= 0)
            vert_gap = query_block[:, None] - jnp.repeat(vert_block, BLOCK)[None, :]
            vert_allowed = (vert_gap > 0) & jnp.logical_not(band_member(vert_gap, offsets))
            allowed = jnp.concatenate([band_allowed, vert_allowed], axis=1)
            query_set = query_rows[:, kv_head * per_group:(kv_head + 1) * per_group].astype(jnp.float32)
            scores = jnp.einsum("qgd,kd->qgk", query_set, key_set) * score_scale
            scores = jnp.where(allowed[:, None, :], scores, -1e30)
            row_max = jnp.max(scores, axis=-1)
            weights = jnp.where(allowed[:, None, :], jnp.exp(scores - row_max[..., None]), 0.0)
            row_sum = jnp.sum(weights, axis=-1)
            rounded = lax.optimization_barrier(weights.astype(jnp.bfloat16))
            mixture = jnp.einsum("qgk,kd->qgd", rounded.astype(jnp.float32), value_set)
            attended = (mixture / row_sum[..., None]).astype(jnp.bfloat16).reshape(TOK_DEV, per_group * HEAD)
            proj_rows = out_weight[kv_head * per_group * HEAD:(kv_head + 1) * per_group * HEAD]
            partial_value = jnp.dot(attended, proj_rows, preferred_element_type=jnp.float32).astype(jnp.bfloat16)
            partial_sum = partial_sum + partial_value.astype(jnp.float32)
        return partial_sum.astype(jnp.bfloat16)

    shards = lax.map(shard_output, jnp.arange(N_CTX, dtype=jnp.int32))
    return shards.reshape(SEQ, D)
```

```python
import functools
import math

import jax
import jax.numpy as jnp
from jax import lax
from jax.experimental import pallas as pl
from jax.experimental.pallas import tpu as pltpu
from jax.sharding import PartitionSpec as P

BLOCK = 64
BAND = 3
NEG = -1e30


def shifted(value, axis, steps):
    count = lax.axis_size(axis)
    return lax.ppermute(value, axis, [(source, source + steps) for source in range(count - steps)])


def swapped(value, flip):
    count = lax.axis_size("heads")
    return lax.ppermute(value, "heads", [(source, source ^ flip) for source in range(count)])


def attend_rows(cfg, info, q_ref, win, tiles, gathered, row, first_block, store):
    slash, n_vert, blocks, heads_here, head = cfg
    shard = info[slash + n_vert]
    local = first_block + row
    own = shard * blocks + local
    base = (shard - BAND) * blocks
    count = slash + n_vert
    allowed = []
    for slot in range(slash):
        if slot == 0:
            source = BAND * blocks + local
            allowed.append(None)
        else:
            offset = info[slot]
            offset = jnp.where(offset == 0, info[0], offset)
            source = BAND * blocks + local - offset
            allowed.append(own - offset >= 0)
        gathered[slot * BLOCK : (slot + 1) * BLOCK, :] = win[pl.ds(pl.multiple_of(source * BLOCK, BLOCK), BLOCK), :]
    for shard_from in range(n_vert):
        slot = slash + shard_from
        column = shard_from * blocks + info[slot]
        gap = own - column
        fine = gap > 0
        for other in range(slash):
            fine = jnp.logical_and(fine, gap != info[other])
        allowed.append(fine)
        if tiles is None:
            source = jnp.where(shard - shard_from == BAND, (BAND + 1) * blocks, column - base)
            source = jnp.where(fine, source, BAND * blocks + local)
            piece = win[pl.ds(pl.multiple_of(source * BLOCK, BLOCK), BLOCK), :]
        else:
            piece = tiles[shard_from * BLOCK : (shard_from + 1) * BLOCK, :]
        gathered[slot * BLOCK : (slot + 1) * BLOCK, :] = piece
    lane = lax.broadcasted_iota(jnp.int32, (1, count * BLOCK), 1) // BLOCK
    bias = jnp.zeros((1, count * BLOCK), jnp.float32)
    for slot in range(1, count):
        bias = jnp.where(lane == slot, jnp.where(allowed[slot], 0.0, NEG), bias)
    rows = heads_here * BLOCK
    keys = gathered[:, :head]
    values = gathered[:, head:]
    q = q_ref[row]
    scores = lax.dot_general(q, keys, (((1,), (1,)), ((), ())), preferred_element_type=jnp.float32)
    scores = scores + bias
    col = lax.broadcasted_iota(jnp.int32, (BLOCK, 2 * BLOCK), 1)
    line = lax.broadcasted_iota(jnp.int32, (BLOCK, 2 * BLOCK), 0)
    causal = jnp.where(jnp.logical_or(col <= line, col >= BLOCK), 0.0, NEG)
    causal = jnp.concatenate([causal] * heads_here, axis=0)
    scores = jnp.concatenate([scores[:, : 2 * BLOCK] + causal, scores[:, 2 * BLOCK :]], axis=1)
    factor = math.log2(math.e) * head ** (-0.5)
    row_max = jnp.max(scores, axis=1, keepdims=True)
    weights = jnp.exp2((scores - row_max) * factor).astype(jnp.bfloat16)
    extended = jnp.concatenate([values, jnp.ones_like(values)], axis=1)
    mixed = lax.dot_general(weights, extended, (((1,), (0,)), ((), ())), preferred_element_type=jnp.float32)
    result = (mixed[:, :head] / mixed[:, head:]).astype(jnp.bfloat16)
    for h in range(heads_here):
        store(row, h, result[h * BLOCK : (h + 1) * BLOCK])


def attention_body(cfg, first_block, loads, n_kv, with_tiles, *refs):
    slash, n_vert, blocks, heads_here, head = cfg
    info = refs[0]
    q_ref = refs[1]
    weight = refs[2]
    pieces = refs[3 : 3 + n_kv]
    tiles = refs[3 + n_kv]
    attended, keep, send = refs[4 + n_kv : 7 + n_kv]
    win, gathered, w_keep, w_send, sems, w_sems = refs[7 + n_kv :]
    width = keep.shape[1]
    keep_col = info[slash + n_vert + 1]
    send_col = info[slash + n_vert + 2]
    w_copies = [
        pltpu.make_async_copy(weight.at[:, pl.ds(pl.multiple_of(keep_col * width, 128), width)], w_keep, w_sems.at[0]),
        pltpu.make_async_copy(weight.at[:, pl.ds(pl.multiple_of(send_col * width, 128), width)], w_send, w_sems.at[1]),
    ]
    copies = []
    for index, (piece, at) in enumerate(zip(pieces, loads)):
        copies.append(pltpu.make_async_copy(piece, win.at[at : at + piece.shape[0]], sems.at[index]))
    if not with_tiles:
        at = (BAND + 1) * blocks * BLOCK
        copies.append(pltpu.make_async_copy(tiles, win.at[at : at + BLOCK], sems.at[n_kv]))
    for copy in copies:
        copy.start()
    for copy in w_copies:
        copy.start()
    for copy in copies:
        copy.wait()

    def store(row, h, value):
        attended[row * BLOCK : (row + 1) * BLOCK, h * head : (h + 1) * head] = value

    for row in range(q_ref.shape[0]):
        attend_rows(cfg, info, q_ref, win, tiles if with_tiles else None, gathered, row, first_block, store)
    for copy in w_copies:
        copy.wait()
    send[...] = jnp.dot(attended[...], w_send[...], preferred_element_type=jnp.float32).astype(send.dtype)
    keep[...] = jnp.dot(attended[...], w_keep[...], preferred_element_type=jnp.float32).astype(keep.dtype)


def attention(cfg, info, q, weight, pieces, loads, tiles, first_block, with_tiles):
    slash, n_vert, blocks, heads_here, head = cfg
    rows = q.shape[0] * BLOCK
    width = weight.shape[1] // 4
    count = slash + n_vert
    n_kv = len(pieces)
    vmem = pl.BlockSpec(memory_space=pltpu.VMEM)
    anywhere = pl.BlockSpec(memory_space=pl.ANY)
    out = jax.ShapeDtypeStruct((rows, width), jnp.bfloat16)
    return pl.pallas_call(
        functools.partial(attention_body, cfg, first_block, loads, n_kv, with_tiles),
        out_shape=[jax.ShapeDtypeStruct((rows, heads_here * head), jnp.bfloat16), out, out],
        in_specs=[pl.BlockSpec(memory_space=pltpu.SMEM), vmem, anywhere]
        + [anywhere] * n_kv
        + [vmem if with_tiles else anywhere],
        out_specs=[vmem] * 3,
        scratch_shapes=[
            pltpu.VMEM((((BAND + 1) * blocks + 1) * BLOCK, 2 * head), jnp.bfloat16),
            pltpu.VMEM((count * BLOCK, 2 * head), jnp.bfloat16),
            pltpu.VMEM((weight.shape[0], width), jnp.bfloat16),
            pltpu.VMEM((weight.shape[0], width), jnp.bfloat16),
            pltpu.SemaphoreType.DMA((n_kv + 1,)),
            pltpu.SemaphoreType.DMA((2,)),
        ],
        compiler_params=pltpu.CompilerParams(vmem_limit_bytes=40 * 1024 * 1024),
        cost_estimate=pl.CostEstimate(flops=2 * rows * heads_here * head * (2 * width + 4 * count * BLOCK), bytes_accessed=6_000_000, transcendentals=rows * heads_here * count * BLOCK),
        name="attend",
    )(info, q, weight, *pieces, tiles)


def project_body(info, at_low, at_high, weight, keep, send, w_keep, w_send, w_sems):
    width = keep.shape[1]
    rows = at_low.shape[0]
    last = info.shape[0] - 1
    copies = [
        pltpu.make_async_copy(weight.at[:, pl.ds(pl.multiple_of(info[last - 1] * width, 128), width)], w_keep, w_sems.at[0]),
        pltpu.make_async_copy(weight.at[:, pl.ds(pl.multiple_of(info[last] * width, 128), width)], w_send, w_sems.at[1]),
    ]
    for copy in copies:
        copy.start()
    for copy in copies:
        copy.wait()
    for part, source in ((0, at_low), (1, at_high)):
        where = slice(part * rows, (part + 1) * rows)
        send[where, :] = jnp.dot(source[...], w_send[...], preferred_element_type=jnp.float32).astype(send.dtype)
        keep[where, :] = jnp.dot(source[...], w_keep[...], preferred_element_type=jnp.float32).astype(keep.dtype)


def project(info, at_low, at_high, weight):
    rows = at_low.shape[0] * 2
    width = weight.shape[1] // 4
    vmem = pl.BlockSpec(memory_space=pltpu.VMEM)
    out = jax.ShapeDtypeStruct((rows, width), jnp.bfloat16)
    return pl.pallas_call(
        project_body,
        out_shape=[out, out],
        in_specs=[pl.BlockSpec(memory_space=pltpu.SMEM), vmem, vmem, pl.BlockSpec(memory_space=pl.ANY)],
        out_specs=[vmem] * 2,
        scratch_shapes=[
            pltpu.VMEM((weight.shape[0], width), jnp.bfloat16),
            pltpu.VMEM((weight.shape[0], width), jnp.bfloat16),
            pltpu.SemaphoreType.DMA((2,)),
        ],
        compiler_params=pltpu.CompilerParams(vmem_limit_bytes=40 * 1024 * 1024),
        cost_estimate=pl.CostEstimate(flops=4 * rows * weight.shape[0] * width, bytes_accessed=6_000_000, transcendentals=0),
        name="project",
    )(info, at_low, at_high, weight)


def on_device(queries, key_states, value_states, out_weight, slash_offsets, vertical_blocks):
    rows_here, per_group, head = queries.shape
    blocks = rows_here // BLOCK
    half = rows_here // 2
    slash = slash_offsets.shape[1]
    shard = lax.axis_index("ctx")
    ctx_count = lax.axis_size("ctx")
    place = lax.axis_index("heads")
    cfg = (slash, ctx_count, blocks, per_group, head)

    kv = jnp.concatenate([key_states[:, 0, :], value_states[:, 0, :]], axis=1)
    low, high = [kv[:half]], [kv[half:]]
    for _ in range(BAND):
        high.append(shifted(high[-1], "ctx", 1))
        low.append(shifted(low[-1], "ctx", 1))
    own_vertical = lax.dynamic_index_in_dim(vertical_blocks[0], shard, 0, keepdims=False)
    tile = lax.dynamic_slice_in_dim(kv, own_vertical * BLOCK, BLOCK, 0)
    with_tiles = ctx_count > BAND + 1
    if with_tiles:
        tiles = lax.all_gather(tile, "ctx", axis=0, tiled=True)
    else:
        tiles = shifted(tile, "ctx", BAND)

    q = queries.reshape(blocks, BLOCK, per_group, head).transpose(0, 2, 1, 3)
    q = q.reshape(blocks, per_group * BLOCK, head)

    far_keep = place ^ 2
    far_send = place ^ 3
    position = jnp.concatenate([slash_offsets[0], vertical_blocks[0]])
    info_far = jnp.concatenate([position, jnp.stack([shard, far_keep, far_send]).astype(jnp.int32)])
    info_near = jnp.stack([place, place ^ 1]).astype(jnp.int32)

    def window(parts):
        pieces, loads = [], []
        for stride, part in parts:
            pieces.append((low, high)[part][stride])
            loads.append((BAND - stride) * rows_here + part * half)
        return pieces, loads

    upper = window([(3, 1), (2, 0), (2, 1), (1, 0), (1, 1), (0, 0), (0, 1)])
    lower = window([(3, 0), (3, 1), (2, 0), (2, 1), (1, 0), (1, 1), (0, 0)])
    mid = blocks // 2
    att_high, keep_high, send_high = attention(cfg, info_far, q[mid:], out_weight, *upper, tiles, mid, with_tiles)
    from_core_high = swapped(send_high, 1)
    across_high = swapped(keep_high + from_core_high, 2)
    att_low, keep_low, send_low = attention(cfg, info_far, q[:mid], out_weight, *lower, tiles, 0, with_tiles)
    from_core_low = swapped(send_low, 1)
    across_low = swapped(keep_low + from_core_low, 2)
    keep, send = project(info_near, att_low, att_high, out_weight)
    from_core = swapped(send, 1)
    across = jnp.concatenate([across_low, across_high], axis=0).astype(jnp.float32)
    total = keep.astype(jnp.float32) + from_core.astype(jnp.float32) + across
    return total.astype(jnp.bfloat16)


def solution(mesh):
    placed = (
        P(("groups", "ctx"), "heads", None),
        P(("groups", "ctx"), "heads", None),
        P(("groups", "ctx"), "heads", None),
        P("heads", None),
        P(("groups", "heads"), None),
        P(("groups", "heads"), None),
    )
    return jax.shard_map(
        on_device,
        mesh=mesh,
        in_specs=placed,
        out_specs=P(("groups", "ctx"), "heads"),
        check_vma=False,
    )
```

```python
import functools
import math

import jax
import jax.numpy as jnp
from jax import lax
from jax.experimental import pallas as pl
from jax.experimental.pallas import tpu as pltpu
from jax.sharding import PartitionSpec as P

BLOCK = 64
BAND = 3
NEG = -1e30
VMEM_LIMIT = 12 * 1024 * 1024
COST = pl.CostEstimate(flops=1, bytes_accessed=1, transcendentals=0)
HBM = pl.BlockSpec(memory_space=pltpu.HBM)
VMEM = pl.BlockSpec(memory_space=pltpu.VMEM)
SMEM = pl.BlockSpec(memory_space=pltpu.SMEM)


def shifted(value, axis, steps):
    count = lax.axis_size(axis)
    return lax.ppermute(value, axis, [(source, source + steps) for source in range(count - steps)])


def swapped(value, flip):
    count = lax.axis_size("heads")
    return lax.ppermute(value, "heads", [(source, source ^ flip) for source in range(count)])


def pack_body(keys, values, whole):
    head = keys.shape[1]
    whole[:, :head] = keys[...]
    whole[:, head:] = values[...]


def pack(keys, values):
    rows, head = keys.shape
    return pl.pallas_call(
        pack_body,
        out_shape=jax.ShapeDtypeStruct((rows, 2 * head), keys.dtype),
        in_specs=[VMEM, VMEM],
        out_specs=VMEM,
        compiler_params=pltpu.CompilerParams(vmem_limit_bytes=VMEM_LIMIT),
        cost_estimate=COST,
        name="pack",
    )(keys, values)


def attend_block(cfg, info, q_ref, win, tiles, gathered, local, store):
    slash, n_vert, blocks, heads_here, head = cfg
    shard = lax.axis_index("ctx")
    own = shard * blocks + local
    base = (shard - BAND) * blocks
    count = slash + n_vert
    rows = heads_here * BLOCK
    allowed = []
    for slot in range(slash):
        if slot == 0:
            source = BAND * blocks + local
            allowed.append(None)
        else:
            offset = info[slot]
            offset = jnp.where(offset == 0, info[0], offset)
            source = BAND * blocks + local - offset
            allowed.append(own - offset >= 0)
        piece = win[pl.ds(pl.multiple_of(source * BLOCK, BLOCK), BLOCK), :]
        gathered[slot * BLOCK : (slot + 1) * BLOCK, : 2 * head] = piece
    for shard_from in range(n_vert):
        slot = slash + shard_from
        column = shard_from * blocks + info[slot]
        gap = own - column
        fine = gap > 0
        for other in range(slash):
            fine = jnp.logical_and(fine, gap != info[other])
        allowed.append(fine)
        if tiles is None:
            source = jnp.where(fine, column - base, BAND * blocks + local)
            piece = win[pl.ds(pl.multiple_of(source * BLOCK, BLOCK), BLOCK), :]
        else:
            piece = tiles[shard_from * BLOCK : (shard_from + 1) * BLOCK, :]
        gathered[slot * BLOCK : (slot + 1) * BLOCK, : 2 * head] = piece
    lane = lax.broadcasted_iota(jnp.int32, (1, count * BLOCK), 1) // BLOCK
    bias = jnp.zeros((1, count * BLOCK), jnp.float32)
    for slot in range(1, count):
        bias = jnp.where(lane == slot, jnp.where(allowed[slot], 0.0, NEG), bias)
    col = lax.broadcasted_iota(jnp.int32, (BLOCK, 2 * BLOCK), 1)
    line = lax.broadcasted_iota(jnp.int32, (BLOCK, 2 * BLOCK), 0)
    near = jnp.where(jnp.logical_or(col <= line, col >= BLOCK), bias[:, : 2 * BLOCK], NEG)
    near = jnp.concatenate([near] * heads_here, axis=0)
    q = q_ref[:, local * BLOCK : (local + 1) * BLOCK, :].reshape(rows, head)
    scores = lax.dot_general(q, gathered[:, :head], (((1,), (1,)), ((), ())), preferred_element_type=jnp.float32)
    scores = jnp.concatenate([scores[:, : 2 * BLOCK] + near, scores[:, 2 * BLOCK :] + bias[:, 2 * BLOCK :]], axis=1)
    factor = math.log2(math.e) * head ** (-0.5)
    row_max = jnp.max(scores, axis=1, keepdims=True)
    weights = jnp.exp2((scores - row_max) * factor).astype(jnp.bfloat16)
    mixed = lax.dot_general(weights, gathered[:, head:], (((1,), (0,)), ((), ())), preferred_element_type=jnp.float32)
    result = (mixed[:, :head] / mixed[:, head:]).astype(jnp.bfloat16)
    for h in range(heads_here):
        store(h, result[h * BLOCK : (h + 1) * BLOCK])


def weight_columns(weight, block, width):
    return weight.at[:, pl.ds(pl.multiple_of(block * width, 128), width)]


def matmul(left, right, out):
    out[...] = jnp.dot(left[...], right[...], preferred_element_type=jnp.float32).astype(out.dtype)


def attend_rows(cfg, info, q_ref, win, tiles, gathered, first, attended):
    slash, n_vert, blocks, heads_here, head = cfg
    for index in range(attended.shape[0] // BLOCK):

        def store(h, value):
            attended[index * BLOCK : (index + 1) * BLOCK, h * head : (h + 1) * head] = value

        part = gathered.at[index % gathered.shape[0]]
        attend_block(cfg, info, q_ref, win, tiles, part, first + index, store)


def fill_ones(gathered, head):
    for slot in range(gathered.shape[0]):
        gathered[slot, :, 2 * head :] = jnp.ones((gathered.shape[1], head), jnp.bfloat16)


def early_body(cfg, first, n_pieces, info, q_ref, w_send, *refs):
    head = cfg[-1]
    pieces = refs[:n_pieces]
    tiles = refs[n_pieces] if len(refs) > n_pieces + 5 else None
    attended, send, win, gathered, sems = refs[-5:]
    rows = pieces[0].shape[0]
    copies = []
    for index, piece in enumerate(pieces):
        copies.append(pltpu.make_async_copy(piece, win.at[index * rows : (index + 1) * rows, :], sems.at[index]))
    for copy in copies:
        copy.start()
    fill_ones(gathered, head)
    for copy in copies:
        copy.wait()
    attend_rows(cfg, info, q_ref, win, tiles, gathered, first, attended)
    matmul(attended, w_send, send)


def late_body(cfg, info, q_ref, w_send, w_keep, win, early, *refs):
    head = cfg[-1]
    tiles = refs[0] if len(refs) > 5 else None
    attended, send, keep, keep_early, gathered = refs[-5:]
    fill_ones(gathered, head)
    attend_rows(cfg, info, q_ref, win, tiles, gathered, 0, attended)
    matmul(attended, w_send, send)
    matmul(early, w_keep, keep_early)
    matmul(attended, w_keep, keep)


def rows_of(count, like):
    return jax.ShapeDtypeStruct((count, like), jnp.bfloat16)


def kernel_params(tiles):
    return dict(
        compiler_params=pltpu.CompilerParams(vmem_limit_bytes=4 * VMEM_LIMIT if tiles else VMEM_LIMIT),
        cost_estimate=COST,
    )


def gather_scratch(cfg):
    return pltpu.VMEM((2, (cfg[0] + cfg[1]) * BLOCK, 3 * cfg[-1]), jnp.bfloat16)


def attend_early(cfg, first, info, q, w_send, pieces, tiles):
    slash, n_vert, blocks, heads_here, head = cfg
    rows = (blocks - first) * BLOCK
    return pl.pallas_call(
        functools.partial(early_body, cfg, first, len(pieces)),
        out_shape=[rows_of(rows, heads_here * head), rows_of(rows, w_send.shape[1]), rows_of((BAND + 1) * blocks * BLOCK, 2 * head)],
        in_specs=[SMEM, VMEM, VMEM] + [HBM] * len(pieces) + [VMEM] * len(tiles),
        out_specs=[VMEM] * 3,
        scratch_shapes=[gather_scratch(cfg), pltpu.SemaphoreType.DMA((len(pieces),))],
        name="attend_early",
        **kernel_params(tiles),
    )(info, q, w_send, *pieces, *tiles)


def attend_late(cfg, count, info, q, w_send, w_keep, win, early, tiles):
    slash, n_vert, blocks, heads_here, head = cfg
    rows = count * BLOCK
    width = w_send.shape[1]
    return pl.pallas_call(
        functools.partial(late_body, cfg),
        out_shape=[rows_of(rows, heads_here * head), rows_of(rows, width), rows_of(rows, width), rows_of(early.shape[0], width)],
        in_specs=[SMEM] + [VMEM] * (5 + len(tiles)),
        out_specs=[VMEM] * 4,
        scratch_shapes=[gather_scratch(cfg)],
        name="attend_late",
        **kernel_params(tiles),
    )(info, q, w_send, w_keep, win, early, *tiles)


def stage_body(queries, weight, first, q, *refs):
    slots, sems = refs[:4], refs[4]
    width = slots[0].shape[1]
    place = lax.axis_index("heads")
    copies = [pltpu.make_async_copy(queries, q, sems.at[0])]
    for index, flip in enumerate((3, 2, 1, 0)):
        copies.append(pltpu.make_async_copy(weight_columns(weight, place ^ flip, width), slots[index], sems.at[1 + index]))
    for copy in copies:
        copy.start()
    for copy in copies:
        copy.wait()


def stage(q, weight, first):
    part = jax.ShapeDtypeStruct((weight.shape[0], weight.shape[1] // 4), weight.dtype)
    return pl.pallas_call(
        stage_body,
        out_shape=[jax.ShapeDtypeStruct(q.shape, q.dtype)] + [part] * 4,
        in_specs=[HBM] * 3,
        out_specs=[VMEM] * 5,
        scratch_shapes=[pltpu.SemaphoreType.DMA((5,))],
        compiler_params=pltpu.CompilerParams(vmem_limit_bytes=VMEM_LIMIT),
        cost_estimate=COST,
        name="stage",
    )(q, weight, first)


def project_body(late, early, w_send, w_keep, after, send, keep):
    rows = late.shape[0]
    for at, source in ((slice(0, rows), late), (slice(rows, send.shape[0]), early)):
        matmul(source, w_send, send.at[at, :])
        matmul(source, w_keep, keep.at[at, :])


def project(late, early, w_send, w_keep, after):
    rows = late.shape[0] + early.shape[0]
    return pl.pallas_call(
        project_body,
        out_shape=[rows_of(rows, w_send.shape[1])] * 2,
        in_specs=[VMEM] * 4 + [HBM],
        out_specs=[VMEM] * 2,
        compiler_params=pltpu.CompilerParams(vmem_limit_bytes=VMEM_LIMIT),
        cost_estimate=COST,
        name="project",
    )(late, early, w_send, w_keep, after)


def finish_body(at, near, other, across, *refs):
    out, total, sem = refs[-3:]
    rows = total.shape[0]
    where = slice(at, at + rows)
    value = near[where, :].astype(jnp.float32) + other[where, :].astype(jnp.float32) + across[...].astype(jnp.float32)
    total[...] = value.astype(total.dtype)
    copy = pltpu.make_async_copy(total, out.at[where, :], sem)
    copy.start()
    copy.wait()


def finish(near, other, across, at, before=None):
    held = [] if before is None else [before]
    return pl.pallas_call(
        functools.partial(finish_body, at),
        out_shape=rows_of(*near.shape),
        in_specs=[VMEM] * 3 + [HBM] * len(held),
        out_specs=HBM,
        scratch_shapes=[pltpu.VMEM(across.shape, across.dtype), pltpu.SemaphoreType.DMA],
        input_output_aliases={3: 0} if held else {},
        compiler_params=pltpu.CompilerParams(vmem_limit_bytes=VMEM_LIMIT),
        cost_estimate=COST,
        name="finish",
    )(near, other, across, *held)


def on_device(queries, key_states, value_states, out_weight, slash_offsets, vertical_blocks):
    rows_here, per_group, head = queries.shape
    blocks = rows_here // BLOCK
    late_blocks = blocks // 2
    ctx_count = lax.axis_size("ctx")
    cfg = (slash_offsets.shape[1], ctx_count, blocks, per_group, head)

    whole = pack(key_states[:, 0, :], value_states[:, 0, :])
    pieces = [shifted(whole, "ctx", stride) for stride in range(BAND, 0, -1)] + [whole]
    q, w_far_send, w_far_keep, w_near_send, w_near_keep = stage(queries.transpose(1, 0, 2), out_weight, whole)
    tiles = []
    if ctx_count > BAND + 1:
        start = lax.dynamic_index_in_dim(vertical_blocks[0], lax.axis_index("ctx"), 0, keepdims=False) * BLOCK
        tile = lax.dynamic_slice_in_dim(whole, start, BLOCK, 0)
        tiles.append(lax.all_gather(tile, "ctx", axis=0, tiled=True))
    info = jnp.concatenate([slash_offsets[0], vertical_blocks[0]])

    early, send, win = attend_early(cfg, late_blocks, info, q, w_far_send, pieces, tiles)
    core_early = swapped(send, 1)
    late, send, keep_late, keep_early = attend_late(cfg, late_blocks, info, q, w_far_send, w_far_keep, win, early, tiles)
    core_late = swapped(send, 1)
    across_early = swapped(keep_early + core_early, 2)
    mine_late = keep_late + core_late
    across_late = swapped(mine_late, 2)
    near_send, near_keep = project(late, early, w_near_send, w_near_keep, mine_late)
    core_near = swapped(near_send, 1)
    out = finish(near_keep, core_near, across_early, late_blocks * BLOCK)
    return finish(near_keep, core_near, across_late, 0, out)


def solution(mesh):
    placed = (
        P(("groups", "ctx"), "heads", None),
        P(("groups", "ctx"), "heads", None),
        P(("groups", "ctx"), "heads", None),
        P("heads", None),
        P(("groups", "heads"), None),
        P(("groups", "heads"), None),
    )
    return jax.shard_map(
        on_device,
        mesh=mesh,
        in_specs=placed,
        out_specs=P(("groups", "ctx"), "heads"),
        check_vma=False,
    )
```

```python
import functools
import math

import jax
import jax.numpy as jnp
from jax import lax
from jax.experimental import pallas as pl
from jax.experimental.pallas import tpu as pltpu
from jax.sharding import PartitionSpec as P

BLOCK = 64
BAND = 3
NEG = -1e30
VMEM_LIMIT = 12 * 1024 * 1024
COST = pl.CostEstimate(flops=1, bytes_accessed=1, transcendentals=0)
HBM = pl.BlockSpec(memory_space=pltpu.HBM)
VMEM = pl.BlockSpec(memory_space=pltpu.VMEM)
SMEM = pl.BlockSpec(memory_space=pltpu.SMEM)


def shifted(value, axis, steps):
    count = lax.axis_size(axis)
    return lax.ppermute(value, axis, [(source, source + steps) for source in range(count - steps)])


def swapped(value, flip):
    count = lax.axis_size("heads")
    return lax.ppermute(value, "heads", [(source, source ^ flip) for source in range(count)])


def attend_block(cfg, info, q_ref, win, tiles, gathered, local, store):
    slash, n_vert, blocks, heads_here, head = cfg
    shard = lax.axis_index("ctx")
    own = shard * blocks + local
    base = (shard - BAND) * blocks
    count = slash + n_vert
    rows = heads_here * BLOCK
    allowed = []
    for slot in range(slash):
        if slot == 0:
            source = BAND * blocks + local
            allowed.append(None)
        else:
            offset = info[slot]
            offset = jnp.where(offset == 0, info[0], offset)
            source = BAND * blocks + local - offset
            allowed.append(own - offset >= 0)
        piece = win[pl.ds(pl.multiple_of(source * BLOCK, BLOCK), BLOCK), :]
        gathered[slot * BLOCK : (slot + 1) * BLOCK, : 2 * head] = piece
    for shard_from in range(n_vert):
        slot = slash + shard_from
        column = shard_from * blocks + info[slot]
        gap = own - column
        fine = gap > 0
        for other in range(slash):
            fine = jnp.logical_and(fine, gap != info[other])
        allowed.append(fine)
        if tiles is None:
            source = jnp.where(fine, column - base, BAND * blocks + local)
            piece = win[pl.ds(pl.multiple_of(source * BLOCK, BLOCK), BLOCK), :]
        else:
            piece = tiles[shard_from * BLOCK : (shard_from + 1) * BLOCK, :]
        gathered[slot * BLOCK : (slot + 1) * BLOCK, : 2 * head] = piece
    lane = lax.broadcasted_iota(jnp.int32, (1, count * BLOCK), 1) // BLOCK
    bias = jnp.zeros((1, count * BLOCK), jnp.float32)
    for slot in range(1, count):
        bias = jnp.where(lane == slot, jnp.where(allowed[slot], 0.0, NEG), bias)
    col = lax.broadcasted_iota(jnp.int32, (BLOCK, 2 * BLOCK), 1)
    line = lax.broadcasted_iota(jnp.int32, (BLOCK, 2 * BLOCK), 0)
    near = jnp.where(jnp.logical_or(col <= line, col >= BLOCK), bias[:, : 2 * BLOCK], NEG)
    near = jnp.concatenate([near] * heads_here, axis=0)
    q = q_ref[:, local * BLOCK : (local + 1) * BLOCK, :].reshape(rows, head)
    scores = lax.dot_general(q, gathered[:, :head], (((1,), (1,)), ((), ())), preferred_element_type=jnp.float32)
    scores = jnp.concatenate([scores[:, : 2 * BLOCK] + near, scores[:, 2 * BLOCK :] + bias[:, 2 * BLOCK :]], axis=1)
    factor = math.log2(math.e) * head ** (-0.5)
    row_max = jnp.max(scores, axis=1, keepdims=True)
    weights = jnp.exp2((scores - row_max) * factor).astype(jnp.bfloat16)
    mixed = lax.dot_general(weights, gathered[:, head:], (((1,), (0,)), ((), ())), preferred_element_type=jnp.float32)
    result = (mixed[:, :head] / mixed[:, head:]).astype(jnp.bfloat16)
    for h in range(heads_here):
        store(h, result[h * BLOCK : (h + 1) * BLOCK])


def weight_columns(weight, block, width):
    return weight.at[:, pl.ds(pl.multiple_of(block * width, 128), width)]


def matmul(left, right, out):
    out[...] = jnp.dot(left[...], right[...], preferred_element_type=jnp.float32).astype(out.dtype)


def attend_rows(cfg, info, q_ref, win, tiles, gathered, first, attended):
    slash, n_vert, blocks, heads_here, head = cfg
    for index in range(attended.shape[0] // BLOCK):

        def store(h, value):
            attended[index * BLOCK : (index + 1) * BLOCK, h * head : (h + 1) * head] = value

        part = gathered.at[index % gathered.shape[0]]
        attend_block(cfg, info, q_ref, win, tiles, part, first + index, store)


def fill_ones(gathered, head):
    for slot in range(gathered.shape[0]):
        gathered[slot, :, 2 * head :] = jnp.ones((gathered.shape[1], head), jnp.bfloat16)


def early_body(cfg, first, strides, info, q_ref, w_send, *refs):
    head = cfg[-1]
    n_pieces = len(strides)
    pieces = refs[:n_pieces]
    tiles = refs[n_pieces] if len(refs) > n_pieces + 5 else None
    attended, send, win, gathered, sems = refs[-5:]
    rows = pieces[0].shape[0]
    copies = []
    for index, piece in enumerate(pieces):
        at = (BAND - strides[index]) * rows
        copies.append(pltpu.make_async_copy(piece, win.at[at : at + rows, :], sems.at[index]))
    for copy in copies:
        copy.start()
    fill_ones(gathered, head)
    for copy in copies:
        copy.wait()
    attend_rows(cfg, info, q_ref, win, tiles, gathered, first, attended)
    matmul(attended, w_send, send)


def late_body(cfg, info, q_ref, w_send, w_keep, win, early, *refs):
    head = cfg[-1]
    tiles = refs[0] if len(refs) > 5 else None
    attended, send, keep, keep_early, gathered = refs[-5:]
    fill_ones(gathered, head)
    attend_rows(cfg, info, q_ref, win, tiles, gathered, 0, attended)
    matmul(attended, w_send, send)
    matmul(early, w_keep, keep_early)
    matmul(attended, w_keep, keep)


def rows_of(count, like):
    return jax.ShapeDtypeStruct((count, like), jnp.bfloat16)


def kernel_params(tiles, rows):
    return dict(
        compiler_params=pltpu.CompilerParams(vmem_limit_bytes=4 * VMEM_LIMIT if tiles else VMEM_LIMIT),
        cost_estimate=pl.CostEstimate(flops=8_000_000 * rows, bytes_accessed=6_000_000, transcendentals=6000 * rows),
    )


def gather_scratch(cfg):
    return pltpu.VMEM((2, (cfg[0] + cfg[1]) * BLOCK, 3 * cfg[-1]), jnp.bfloat16)


def attend_early(cfg, first, info, q, w_send, pieces, strides, tiles):
    slash, n_vert, blocks, heads_here, head = cfg
    rows = (blocks - first) * BLOCK
    return pl.pallas_call(
        functools.partial(early_body, cfg, first, strides),
        out_shape=[rows_of(rows, heads_here * head), rows_of(rows, w_send.shape[1]), rows_of((BAND + 1) * blocks * BLOCK, 2 * head)],
        in_specs=[SMEM, VMEM, VMEM] + [HBM] * len(pieces) + [VMEM] * len(tiles),
        out_specs=[VMEM] * 3,
        scratch_shapes=[gather_scratch(cfg), pltpu.SemaphoreType.DMA((len(pieces),))],
        name="attend_early",
        **kernel_params(tiles, rows),
    )(info, q, w_send, *pieces, *tiles)


def attend_late(cfg, count, info, q, w_send, w_keep, win, early, tiles):
    slash, n_vert, blocks, heads_here, head = cfg
    rows = count * BLOCK
    width = w_send.shape[1]
    return pl.pallas_call(
        functools.partial(late_body, cfg),
        out_shape=[rows_of(rows, heads_here * head), rows_of(rows, width), rows_of(rows, width), rows_of(early.shape[0], width)],
        in_specs=[SMEM] + [VMEM] * (5 + len(tiles)),
        out_specs=[VMEM] * 4,
        scratch_shapes=[gather_scratch(cfg)],
        name="attend_late",
        **kernel_params(tiles, rows),
    )(info, q, w_send, w_keep, win, early, *tiles)


def stage_body(queries, weight, first, q, *refs):
    slots, sems = refs[:4], refs[4]
    width = slots[0].shape[1]
    place = lax.axis_index("heads")
    copies = [pltpu.make_async_copy(queries, q, sems.at[0])]
    for index, flip in enumerate((3, 2, 1, 0)):
        copies.append(pltpu.make_async_copy(weight_columns(weight, place ^ flip, width), slots[index], sems.at[1 + index]))
    for copy in copies:
        copy.start()
    for copy in copies:
        copy.wait()


def stage(q, weight, first):
    part = jax.ShapeDtypeStruct((weight.shape[0], weight.shape[1] // 4), weight.dtype)
    return pl.pallas_call(
        stage_body,
        out_shape=[jax.ShapeDtypeStruct(q.shape, q.dtype)] + [part] * 4,
        in_specs=[HBM] * 3,
        out_specs=[VMEM] * 5,
        scratch_shapes=[pltpu.SemaphoreType.DMA((5,))],
        compiler_params=pltpu.CompilerParams(vmem_limit_bytes=VMEM_LIMIT),
        cost_estimate=COST,
        name="stage",
    )(q, weight, first)


def join_body(keep_late, core_late, keep_early, core_early, mine):
    rows = keep_late.shape[0]
    for at, one, two in ((0, keep_late, core_late), (rows, keep_early, core_early)):
        total = one[...].astype(jnp.float32) + two[...].astype(jnp.float32)
        mine[at : at + one.shape[0], :] = total.astype(mine.dtype)


def join(keep_late, core_late, keep_early, core_early):
    return pl.pallas_call(
        join_body,
        out_shape=rows_of(keep_late.shape[0] + keep_early.shape[0], keep_late.shape[1]),
        in_specs=[VMEM] * 4,
        out_specs=VMEM,
        compiler_params=pltpu.CompilerParams(vmem_limit_bytes=VMEM_LIMIT),
        cost_estimate=COST,
        name="join",
    )(keep_late, core_late, keep_early, core_early)


def project_body(late, early, w_send, w_keep, after, send_late, send_early, keep_late, keep_early):
    matmul(late, w_send, send_late)
    matmul(early, w_send, send_early)
    matmul(late, w_keep, keep_late)
    matmul(early, w_keep, keep_early)


def project(late, early, w_send, w_keep, after):
    shapes = [rows_of(late.shape[0], w_send.shape[1]), rows_of(early.shape[0], w_send.shape[1])]
    rows = late.shape[0] + early.shape[0]
    return pl.pallas_call(
        project_body,
        out_shape=shapes + shapes,
        in_specs=[VMEM] * 4 + [HBM],
        out_specs=[VMEM] * 4,
        compiler_params=pltpu.CompilerParams(vmem_limit_bytes=VMEM_LIMIT),
        cost_estimate=pl.CostEstimate(flops=3_300_000 * rows, bytes_accessed=6_000_000, transcendentals=0),
        name="project",
    )(late, early, w_send, w_keep, after)


def finish_body(keep_late, keep_early, core_late, core_early, across, out, total, sems):
    rows = keep_late.shape[0]
    copies = []
    for index, (at, one, two) in enumerate(((0, keep_late, core_late), (rows, keep_early, core_early))):
        where = slice(at, at + one.shape[0])
        value = one[...].astype(jnp.float32) + two[...].astype(jnp.float32) + across[where, :].astype(jnp.float32)
        total[where, :] = value.astype(total.dtype)
        copies.append(pltpu.make_async_copy(total.at[where, :], out.at[where, :], sems.at[index]))
        copies[-1].start()
    for copy in copies:
        copy.wait()


def finish(keep_late, keep_early, core_late, core_early, across):
    return pl.pallas_call(
        finish_body,
        out_shape=rows_of(*across.shape),
        in_specs=[VMEM] * 5,
        out_specs=HBM,
        scratch_shapes=[pltpu.VMEM(across.shape, across.dtype), pltpu.SemaphoreType.DMA((2,))],
        compiler_params=pltpu.CompilerParams(vmem_limit_bytes=VMEM_LIMIT),
        cost_estimate=COST,
        name="finish",
    )(keep_late, keep_early, core_late, core_early, across)


def on_device(queries, key_states, value_states, out_weight, slash_offsets, vertical_blocks):
    rows_here, per_group, head = queries.shape
    blocks = rows_here // BLOCK
    late_blocks = blocks // 2
    ctx_count = lax.axis_size("ctx")
    cfg = (slash_offsets.shape[1], ctx_count, blocks, per_group, head)

    strides = (1, 3, 2)
    whole = jnp.concatenate([key_states[:, 0, :], value_states[:, 0, :]], axis=1)
    one = shifted(whole, "ctx", 1)
    three = shifted(whole, "ctx", 3)
    q, w_far_send, w_far_keep, w_near_send, w_near_keep = stage(queries.transpose(1, 0, 2), out_weight, whole)
    one, q = lax.optimization_barrier((one, q))
    pieces = [whole, one, three, shifted(one, "ctx", 1)]
    tiles = []
    if ctx_count > BAND + 1:
        start = lax.dynamic_index_in_dim(vertical_blocks[0], lax.axis_index("ctx"), 0, keepdims=False) * BLOCK
        tile = lax.dynamic_slice_in_dim(whole, start, BLOCK, 0)
        tiles.append(lax.all_gather(tile, "ctx", axis=0, tiled=True))
    info = jnp.concatenate([slash_offsets[0], vertical_blocks[0]])

    early, send, win = attend_early(cfg, late_blocks, info, q, w_far_send, pieces, (0,) + strides, tiles)
    core_early = swapped(send, 1)
    late, send, keep_late, keep_early = attend_late(cfg, late_blocks, info, q, w_far_send, w_far_keep, win, early, tiles)
    core_late = swapped(send, 1)
    mine = join(keep_late, core_late, keep_early, core_early)
    across = swapped(mine, 2)
    send_late, send_early, keep_late, keep_early = project(late, early, w_near_send, w_near_keep, mine)
    return finish(keep_late, keep_early, swapped(send_late, 1), swapped(send_early, 1), across)


def solution(mesh):
    placed = (
        P(("groups", "ctx"), "heads", None),
        P(("groups", "ctx"), "heads", None),
        P(("groups", "ctx"), "heads", None),
        P("heads", None),
        P(("groups", "heads"), None),
        P(("groups", "heads"), None),
    )
    return jax.shard_map(
        on_device,
        mesh=mesh,
        in_specs=placed,
        out_specs=P(("groups", "ctx"), "heads"),
        check_vma=False,
    )
```

```python
import functools
import math

import jax
import jax.numpy as jnp
from jax import lax
from jax.experimental import pallas as pl
from jax.experimental.pallas import tpu as pltpu
from jax.sharding import PartitionSpec as P

BLOCK = 64
BAND = 3
NEG = -1e30
VMEM_LIMIT = 12 * 1024 * 1024
COST = pl.CostEstimate(flops=1, bytes_accessed=1, transcendentals=0)
HBM = pl.BlockSpec(memory_space=pltpu.HBM)
VMEM = pl.BlockSpec(memory_space=pltpu.VMEM)
SMEM = pl.BlockSpec(memory_space=pltpu.SMEM)


def shifted(value, axis, steps):
    count = lax.axis_size(axis)
    return lax.ppermute(value, axis, [(source, source + steps) for source in range(count - steps)])


def swapped(value, flip):
    count = lax.axis_size("heads")
    return lax.ppermute(value, "heads", [(source, source ^ flip) for source in range(count)])


def attend_block(cfg, info, q_ref, win, tiles, gathered, local, store):
    slash, n_vert, blocks, heads_here, head = cfg
    shard = lax.axis_index("ctx")
    own = shard * blocks + local
    base = (shard - BAND) * blocks
    count = slash + n_vert
    rows = heads_here * BLOCK
    allowed = []
    for slot in range(slash):
        if slot == 0:
            source = BAND * blocks + local
            allowed.append(None)
        else:
            offset = info[slot]
            offset = jnp.where(offset == 0, info[0], offset)
            source = BAND * blocks + local - offset
            allowed.append(own - offset >= 0)
        piece = win[pl.ds(pl.multiple_of(source * BLOCK, BLOCK), BLOCK), :]
        gathered[slot * BLOCK : (slot + 1) * BLOCK, : 2 * head] = piece
    for shard_from in range(n_vert):
        slot = slash + shard_from
        column = shard_from * blocks + info[slot]
        gap = own - column
        fine = gap > 0
        for other in range(slash):
            fine = jnp.logical_and(fine, gap != info[other])
        allowed.append(fine)
        if tiles is None:
            source = jnp.where(fine, column - base, BAND * blocks + local)
            piece = win[pl.ds(pl.multiple_of(source * BLOCK, BLOCK), BLOCK), :]
        else:
            piece = tiles[shard_from * BLOCK : (shard_from + 1) * BLOCK, :]
        gathered[slot * BLOCK : (slot + 1) * BLOCK, : 2 * head] = piece
    lane = lax.broadcasted_iota(jnp.int32, (1, count * BLOCK), 1) // BLOCK
    bias = jnp.zeros((1, count * BLOCK), jnp.float32)
    for slot in range(1, count):
        bias = jnp.where(lane == slot, jnp.where(allowed[slot], 0.0, NEG), bias)
    col = lax.broadcasted_iota(jnp.int32, (BLOCK, 2 * BLOCK), 1)
    line = lax.broadcasted_iota(jnp.int32, (BLOCK, 2 * BLOCK), 0)
    near = jnp.where(jnp.logical_or(col <= line, col >= BLOCK), bias[:, : 2 * BLOCK], NEG)
    near = jnp.concatenate([near] * heads_here, axis=0)
    q = q_ref[:, local * BLOCK : (local + 1) * BLOCK, :].reshape(rows, head)
    scores = lax.dot_general(q, gathered[:, :head], (((1,), (1,)), ((), ())), preferred_element_type=jnp.float32)
    scores = jnp.concatenate([scores[:, : 2 * BLOCK] + near, scores[:, 2 * BLOCK :] + bias[:, 2 * BLOCK :]], axis=1)
    factor = math.log2(math.e) * head ** (-0.5)
    row_max = jnp.max(scores, axis=1, keepdims=True)
    weights = jnp.exp2((scores - row_max) * factor).astype(jnp.bfloat16)
    mixed = lax.dot_general(weights, gathered[:, head:], (((1,), (0,)), ((), ())), preferred_element_type=jnp.float32)
    result = (mixed[:, :head] / mixed[:, head:]).astype(jnp.bfloat16)
    for h in range(heads_here):
        store(h, result[h * BLOCK : (h + 1) * BLOCK])


def weight_columns(weight, block, width):
    return weight.at[:, pl.ds(pl.multiple_of(block * width, 128), width)]


def matmul(left, right, out):
    out[...] = jnp.dot(left[...], right[...], preferred_element_type=jnp.float32).astype(out.dtype)


def attend_rows(cfg, info, q_ref, win, tiles, gathered, first, attended):
    slash, n_vert, blocks, heads_here, head = cfg
    for index in range(attended.shape[0] // BLOCK):

        def store(h, value):
            attended[index * BLOCK : (index + 1) * BLOCK, h * head : (h + 1) * head] = value

        part = gathered.at[index % gathered.shape[0]]
        attend_block(cfg, info, q_ref, win, tiles, part, first + index, store)


def fill_ones(gathered, head):
    for slot in range(gathered.shape[0]):
        gathered[slot, :, 2 * head :] = jnp.ones((gathered.shape[1], head), jnp.bfloat16)


def fill_body(strides, *refs):
    win, sems = refs[-2:]
    rows = refs[0].shape[0]
    copies = []
    for index, stride in enumerate(strides):
        at = (BAND - stride) * rows
        copies.append(pltpu.make_async_copy(refs[index], win.at[at : at + rows, :], sems.at[index]))
    for copy in copies:
        copy.start()
    for copy in copies:
        copy.wait()


def fill(pieces, strides):
    rows, width = pieces[0].shape
    return pl.pallas_call(
        functools.partial(fill_body, strides),
        out_shape=rows_of((BAND + 1) * rows, width),
        in_specs=[HBM] * len(pieces),
        out_specs=VMEM,
        scratch_shapes=[pltpu.SemaphoreType.DMA((len(pieces),))],
        compiler_params=pltpu.CompilerParams(vmem_limit_bytes=VMEM_LIMIT),
        cost_estimate=COST,
        name="fill",
    )(*pieces)


def early_body(cfg, first, at, info, q_ref, w_send, held, piece, *refs):
    head = cfg[-1]
    tiles = refs[0] if len(refs) > 5 else None
    attended, send, win, gathered, sem = refs[-5:]
    copy = pltpu.make_async_copy(piece, win.at[at : at + piece.shape[0], :], sem)
    copy.start()
    fill_ones(gathered, head)
    copy.wait()
    attend_rows(cfg, info, q_ref, win, tiles, gathered, first, attended)
    matmul(attended, w_send, send)


def next_body(cfg, first, info, q_ref, w_send, w_keep, win, before, *refs):
    head = cfg[-1]
    tiles = refs[0] if len(refs) > 4 else None
    attended, send, keep, gathered = refs[-4:]
    fill_ones(gathered, head)
    attend_rows(cfg, info, q_ref, win, tiles, gathered, first, attended)
    matmul(attended, w_send, send)
    matmul(before, w_keep, keep)


def rows_of(count, like):
    return jax.ShapeDtypeStruct((count, like), jnp.bfloat16)


def kernel_params(tiles, rows):
    return dict(
        compiler_params=pltpu.CompilerParams(vmem_limit_bytes=4 * VMEM_LIMIT if tiles else VMEM_LIMIT),
        cost_estimate=pl.CostEstimate(flops=8_000_000 * rows, bytes_accessed=6_000_000, transcendentals=6000 * rows),
    )


def gather_scratch(cfg):
    return pltpu.VMEM((2, (cfg[0] + cfg[1]) * BLOCK, 3 * cfg[-1]), jnp.bfloat16)


def attend_early(cfg, first, count, info, q, w_send, win, piece, stride, tiles):
    slash, n_vert, blocks, heads_here, head = cfg
    rows = count * BLOCK
    return pl.pallas_call(
        functools.partial(early_body, cfg, first, (BAND - stride) * piece.shape[0]),
        out_shape=[rows_of(rows, heads_here * head), rows_of(rows, w_send.shape[1]), rows_of(*win.shape)],
        in_specs=[SMEM] + [VMEM] * 3 + [HBM] + [VMEM] * len(tiles),
        out_specs=[VMEM] * 3,
        scratch_shapes=[gather_scratch(cfg), pltpu.SemaphoreType.DMA],
        input_output_aliases={3: 2},
        name="attend_early",
        **kernel_params(tiles, rows),
    )(info, q, w_send, win, piece, *tiles)


def attend_next(cfg, first, count, info, q, w_send, w_keep, win, before, tiles):
    slash, n_vert, blocks, heads_here, head = cfg
    rows = count * BLOCK
    width = w_send.shape[1]
    return pl.pallas_call(
        functools.partial(next_body, cfg, first),
        out_shape=[rows_of(rows, heads_here * head), rows_of(rows, width), rows_of(before.shape[0], width)],
        in_specs=[SMEM] + [VMEM] * (5 + len(tiles)),
        out_specs=[VMEM] * 3,
        scratch_shapes=[gather_scratch(cfg)],
        name="attend_next",
        **kernel_params(tiles, rows),
    )(info, q, w_send, w_keep, win, before, *tiles)


def stage_body(queries, weight, first, q, *refs):
    slots, sems = refs[:4], refs[4]
    width = slots[0].shape[1]
    place = lax.axis_index("heads")
    copies = [pltpu.make_async_copy(queries, q, sems.at[0])]
    for index, flip in enumerate((3, 2, 1, 0)):
        copies.append(pltpu.make_async_copy(weight_columns(weight, place ^ flip, width), slots[index], sems.at[1 + index]))
    for copy in copies:
        copy.start()
    for copy in copies:
        copy.wait()


def stage(q, weight, first):
    part = jax.ShapeDtypeStruct((weight.shape[0], weight.shape[1] // 4), weight.dtype)
    return pl.pallas_call(
        stage_body,
        out_shape=[jax.ShapeDtypeStruct(q.shape, q.dtype)] + [part] * 4,
        in_specs=[HBM] * 3,
        out_specs=[VMEM] * 5,
        scratch_shapes=[pltpu.SemaphoreType.DMA((5,))],
        compiler_params=pltpu.CompilerParams(vmem_limit_bytes=VMEM_LIMIT),
        cost_estimate=COST,
        name="stage",
    )(q, weight, first)


def project_body(count, *refs):
    sources, weights, outs = refs[:count], refs[count:-count], refs[-count:]
    for source, weight, out in zip(sources, weights, outs):
        matmul(source, weight, out)


def project(pairs):
    count = len(pairs)
    flops = sum(2 * source.shape[0] * weight.shape[0] * weight.shape[1] for source, weight in pairs)
    return pl.pallas_call(
        functools.partial(project_body, count),
        out_shape=[rows_of(source.shape[0], weight.shape[1]) for source, weight in pairs],
        in_specs=[VMEM] * (2 * count),
        out_specs=[VMEM] * count,
        compiler_params=pltpu.CompilerParams(vmem_limit_bytes=VMEM_LIMIT),
        cost_estimate=pl.CostEstimate(flops=flops, bytes_accessed=6_000_000, transcendentals=0),
        name="project",
    )(*[source for source, _ in pairs], *[weight for _, weight in pairs])


def finish_body(count, *refs):
    keeps, cores, acrosses = refs[:count], refs[count : 2 * count], refs[2 * count : 3 * count]
    out, total, sems = refs[-3:]
    copies = []
    end = out.shape[0]
    for index in range(count):
        where = slice(end - keeps[index].shape[0], end)
        end = where.start
        value = keeps[index][...].astype(jnp.float32) + cores[index][...].astype(jnp.float32)
        total[where, :] = (value + acrosses[index][...].astype(jnp.float32)).astype(total.dtype)
        copies.append(pltpu.make_async_copy(total.at[where, :], out.at[where, :], sems.at[index]))
        copies[-1].start()
    for copy in copies:
        copy.wait()


def finish(rows, keeps, cores, acrosses):
    width = keeps[0].shape[1]
    count = len(keeps)
    return pl.pallas_call(
        functools.partial(finish_body, count),
        out_shape=rows_of(rows, width),
        in_specs=[VMEM] * (3 * count),
        out_specs=HBM,
        scratch_shapes=[pltpu.VMEM((rows, width), jnp.bfloat16), pltpu.SemaphoreType.DMA((count,))],
        compiler_params=pltpu.CompilerParams(vmem_limit_bytes=VMEM_LIMIT),
        cost_estimate=COST,
        name="finish",
    )(*keeps, *cores, *acrosses)


def on_device(queries, key_states, value_states, out_weight, slash_offsets, vertical_blocks):
    rows_here, per_group, head = queries.shape
    blocks = rows_here // BLOCK
    shares = (3, 3, 2)
    counts = [blocks * share // sum(shares) for share in shares]
    ctx_count = lax.axis_size("ctx")
    cfg = (slash_offsets.shape[1], ctx_count, blocks, per_group, head)

    whole = jnp.concatenate([key_states[:, 0, :], value_states[:, 0, :]], axis=1)
    one = shifted(whole, "ctx", 1)
    three = shifted(whole, "ctx", 3)
    q, w_far_send, w_far_keep, w_near_send, w_near_keep = stage(queries.transpose(1, 0, 2), out_weight, whole)
    one, q = lax.optimization_barrier((one, q))
    two = shifted(one, "ctx", 1)
    win = fill([whole, one, three], (0, 1, BAND))
    tiles = []
    if ctx_count > BAND + 1:
        start = lax.dynamic_index_in_dim(vertical_blocks[0], lax.axis_index("ctx"), 0, keepdims=False) * BLOCK
        tile = lax.dynamic_slice_in_dim(whole, start, BLOCK, 0)
        tiles.append(lax.all_gather(tile, "ctx", axis=0, tiled=True))
    info = jnp.concatenate([slash_offsets[0], vertical_blocks[0]])

    first = blocks - counts[0]
    attended, send, win = attend_early(cfg, first, counts[0], info, q, w_far_send, win, two, 2, tiles)
    sources, cores, acrosses = [attended], [swapped(send, 1)], []
    mine = None
    for count in counts[1:]:
        first -= count
        if mine is not None:
            win, mine = lax.optimization_barrier((win, mine))
            acrosses.append(swapped(mine, 2))
        attended, send, keep = attend_next(cfg, first, count, info, q, w_far_send, w_far_keep, win, sources[-1], tiles)
        mine = keep + cores[-1]
        sources.append(attended)
        cores.append(swapped(send, 1))
    acrosses.append(swapped(mine, 2))
    (keep,) = project([(sources[-1], w_far_keep)])
    mine = keep + cores[-1]
    acrosses.append(swapped(mine, 2))
    acrosses[0], mine, *sources = lax.optimization_barrier((acrosses[0], mine, *sources))
    sends = project([(source, w_near_send) for source in sources])
    keeps = project([(source, w_near_keep) for source in sources])
    return finish(rows_here, keeps, [swapped(send, 1) for send in sends], acrosses)


def solution(mesh):
    placed = (
        P(("groups", "ctx"), "heads", None),
        P(("groups", "ctx"), "heads", None),
        P(("groups", "ctx"), "heads", None),
        P("heads", None),
        P(("groups", "heads"), None),
        P(("groups", "heads"), None),
    )
    return jax.shard_map(
        on_device,
        mesh=mesh,
        in_specs=placed,
        out_specs=P(("groups", "ctx"), "heads"),
        check_vma=False,
    )
```

```python
import functools
import math

import jax
import jax.numpy as jnp
from jax import lax
from jax.experimental import pallas as pl
from jax.experimental.pallas import tpu as pltpu
from jax.sharding import PartitionSpec as P

BLOCK = 64
BAND = 3
NEG = -1e30
VMEM_LIMIT = 12 * 1024 * 1024
COST = pl.CostEstimate(flops=1, bytes_accessed=1, transcendentals=0)
HBM = pl.BlockSpec(memory_space=pltpu.HBM)
VMEM = pl.BlockSpec(memory_space=pltpu.VMEM)
SMEM = pl.BlockSpec(memory_space=pltpu.SMEM)


def shifted(value, axis, steps):
    count = lax.axis_size(axis)
    return lax.ppermute(value, axis, [(source, source + steps) for source in range(count - steps)])


def swapped(value, flip):
    count = lax.axis_size("heads")
    return lax.ppermute(value, "heads", [(source, source ^ flip) for source in range(count)])


def attend_block(cfg, info, q_ref, win, tiles, gathered, local, store):
    slash, n_vert, blocks, heads_here, head = cfg
    shard = lax.axis_index("ctx")
    own = shard * blocks + local
    base = (shard - BAND) * blocks
    count = slash + n_vert
    rows = heads_here * BLOCK
    allowed = []
    for slot in range(slash):
        if slot == 0:
            source = BAND * blocks + local
            allowed.append(None)
        else:
            offset = info[slot]
            offset = jnp.where(offset == 0, info[0], offset)
            source = BAND * blocks + local - offset
            allowed.append(own - offset >= 0)
        piece = win[pl.ds(pl.multiple_of(source * BLOCK, BLOCK), BLOCK), :]
        gathered[slot * BLOCK : (slot + 1) * BLOCK, : 2 * head] = piece
    for shard_from in range(n_vert):
        slot = slash + shard_from
        column = shard_from * blocks + info[slot]
        gap = own - column
        fine = gap > 0
        for other in range(slash):
            fine = jnp.logical_and(fine, gap != info[other])
        allowed.append(fine)
        if tiles is None:
            source = jnp.where(fine, column - base, BAND * blocks + local)
            piece = win[pl.ds(pl.multiple_of(source * BLOCK, BLOCK), BLOCK), :]
        else:
            piece = tiles[shard_from * BLOCK : (shard_from + 1) * BLOCK, :]
        gathered[slot * BLOCK : (slot + 1) * BLOCK, : 2 * head] = piece
    lane = lax.broadcasted_iota(jnp.int32, (1, count * BLOCK), 1) // BLOCK
    bias = jnp.zeros((1, count * BLOCK), jnp.float32)
    for slot in range(1, count):
        bias = jnp.where(lane == slot, jnp.where(allowed[slot], 0.0, NEG), bias)
    col = lax.broadcasted_iota(jnp.int32, (BLOCK, 2 * BLOCK), 1)
    line = lax.broadcasted_iota(jnp.int32, (BLOCK, 2 * BLOCK), 0)
    near = jnp.where(jnp.logical_or(col <= line, col >= BLOCK), bias[:, : 2 * BLOCK], NEG)
    near = jnp.concatenate([near] * heads_here, axis=0)
    q = q_ref[:, local * BLOCK : (local + 1) * BLOCK, :].reshape(rows, head)
    scores = lax.dot_general(q, gathered[:, :head], (((1,), (1,)), ((), ())), preferred_element_type=jnp.float32)
    scores = jnp.concatenate([scores[:, : 2 * BLOCK] + near, scores[:, 2 * BLOCK :] + bias[:, 2 * BLOCK :]], axis=1)
    factor = math.log2(math.e) * head ** (-0.5)
    row_max = jnp.max(scores, axis=1, keepdims=True)
    weights = jnp.exp2((scores - row_max) * factor).astype(jnp.bfloat16)
    mixed = lax.dot_general(weights, gathered[:, head:], (((1,), (0,)), ((), ())), preferred_element_type=jnp.float32)
    result = (mixed[:, :head] / mixed[:, head:]).astype(jnp.bfloat16)
    for h in range(heads_here):
        store(h, result[h * BLOCK : (h + 1) * BLOCK])


def weight_columns(weight, block, width):
    return weight.at[:, pl.ds(pl.multiple_of(block * width, 128), width)]


def matmul(left, right, out):
    out[...] = jnp.dot(left[...], right[...], preferred_element_type=jnp.float32).astype(out.dtype)


def attend_rows(cfg, info, q_ref, win, tiles, gathered, first, attended):
    slash, n_vert, blocks, heads_here, head = cfg
    for index in range(attended.shape[0] // BLOCK):

        def store(h, value):
            attended[index * BLOCK : (index + 1) * BLOCK, h * head : (h + 1) * head] = value

        part = gathered.at[index % gathered.shape[0]]
        attend_block(cfg, info, q_ref, win, tiles, part, first + index, store)


def fill_ones(gathered, head):
    for slot in range(gathered.shape[0]):
        gathered[slot, :, 2 * head :] = jnp.ones((gathered.shape[1], head), jnp.bfloat16)


def fill_body(strides, *refs):
    win, sems = refs[-2:]
    rows = refs[0].shape[0]
    copies = []
    for index, stride in enumerate(strides):
        at = (BAND - stride) * rows
        copies.append(pltpu.make_async_copy(refs[index], win.at[at : at + rows, :], sems.at[index]))
    for copy in copies:
        copy.start()
    for copy in copies:
        copy.wait()


def fill(pieces, strides):
    rows, width = pieces[0].shape
    return pl.pallas_call(
        functools.partial(fill_body, strides),
        out_shape=rows_of((BAND + 1) * rows, width),
        in_specs=[HBM] * len(pieces),
        out_specs=VMEM,
        scratch_shapes=[pltpu.SemaphoreType.DMA((len(pieces),))],
        compiler_params=pltpu.CompilerParams(vmem_limit_bytes=VMEM_LIMIT),
        cost_estimate=COST,
        name="fill",
    )(*pieces)


def early_body(cfg, first, at, info, q_ref, w_send, held, piece, *refs):
    head = cfg[-1]
    tiles = refs[0] if len(refs) > 5 else None
    attended, send, win, gathered, sem = refs[-5:]
    copy = pltpu.make_async_copy(piece, win.at[at : at + piece.shape[0], :], sem)
    copy.start()
    fill_ones(gathered, head)
    copy.wait()
    attend_rows(cfg, info, q_ref, win, tiles, gathered, first, attended)
    matmul(attended, w_send, send)


def next_body(cfg, first, info, q_ref, w_send, w_keep, win, before, *refs):
    head = cfg[-1]
    tiles = refs[0] if len(refs) > 4 else None
    attended, send, keep, gathered = refs[-4:]
    fill_ones(gathered, head)
    attend_rows(cfg, info, q_ref, win, tiles, gathered, first, attended)
    matmul(attended, w_send, send)
    matmul(before, w_keep, keep)


def rows_of(count, like):
    return jax.ShapeDtypeStruct((count, like), jnp.bfloat16)


def kernel_params(tiles, rows):
    return dict(
        compiler_params=pltpu.CompilerParams(vmem_limit_bytes=4 * VMEM_LIMIT if tiles else VMEM_LIMIT),
        cost_estimate=pl.CostEstimate(flops=8_000_000 * rows, bytes_accessed=6_000_000, transcendentals=6000 * rows),
    )


def gather_scratch(cfg):
    return pltpu.VMEM((2, (cfg[0] + cfg[1]) * BLOCK, 3 * cfg[-1]), jnp.bfloat16)


def attend_early(cfg, first, count, info, q, w_send, win, piece, stride, tiles):
    slash, n_vert, blocks, heads_here, head = cfg
    rows = count * BLOCK
    return pl.pallas_call(
        functools.partial(early_body, cfg, first, (BAND - stride) * piece.shape[0]),
        out_shape=[rows_of(rows, heads_here * head), rows_of(rows, w_send.shape[1]), rows_of(*win.shape)],
        in_specs=[SMEM] + [VMEM] * 3 + [HBM] + [VMEM] * len(tiles),
        out_specs=[VMEM] * 3,
        scratch_shapes=[gather_scratch(cfg), pltpu.SemaphoreType.DMA],
        input_output_aliases={3: 2},
        name="attend_early",
        **kernel_params(tiles, rows),
    )(info, q, w_send, win, piece, *tiles)


def attend_next(cfg, first, count, info, q, w_send, w_keep, win, before, tiles):
    slash, n_vert, blocks, heads_here, head = cfg
    rows = count * BLOCK
    width = w_send.shape[1]
    return pl.pallas_call(
        functools.partial(next_body, cfg, first),
        out_shape=[rows_of(rows, heads_here * head), rows_of(rows, width), rows_of(before.shape[0], width)],
        in_specs=[SMEM] + [VMEM] * (5 + len(tiles)),
        out_specs=[VMEM] * 3,
        scratch_shapes=[gather_scratch(cfg)],
        name="attend_next",
        **kernel_params(tiles, rows),
    )(info, q, w_send, w_keep, win, before, *tiles)


def stage_body(queries, weight, first, q, *refs):
    slots, sems = refs[:4], refs[4]
    width = slots[0].shape[1]
    place = lax.axis_index("heads")
    copies = [pltpu.make_async_copy(queries, q, sems.at[0])]
    for index, flip in enumerate((3, 2, 1, 0)):
        copies.append(pltpu.make_async_copy(weight_columns(weight, place ^ flip, width), slots[index], sems.at[1 + index]))
    for copy in copies:
        copy.start()
    for copy in copies:
        copy.wait()


def stage(q, weight, first):
    part = jax.ShapeDtypeStruct((weight.shape[0], weight.shape[1] // 4), weight.dtype)
    return pl.pallas_call(
        stage_body,
        out_shape=[jax.ShapeDtypeStruct(q.shape, q.dtype)] + [part] * 4,
        in_specs=[HBM] * 3,
        out_specs=[VMEM] * 5,
        scratch_shapes=[pltpu.SemaphoreType.DMA((5,))],
        compiler_params=pltpu.CompilerParams(vmem_limit_bytes=VMEM_LIMIT),
        cost_estimate=COST,
        name="stage",
    )(q, weight, first)


def project_body(count, *refs):
    sources, weights, outs = refs[:count], refs[count:-count], refs[-count:]
    for source, weight, out in zip(sources, weights, outs):
        matmul(source, weight, out)


def project(pairs):
    count = len(pairs)
    flops = sum(2 * source.shape[0] * weight.shape[0] * weight.shape[1] for source, weight in pairs)
    return pl.pallas_call(
        functools.partial(project_body, count),
        out_shape=[rows_of(source.shape[0], weight.shape[1]) for source, weight in pairs],
        in_specs=[VMEM] * (2 * count),
        out_specs=[VMEM] * count,
        compiler_params=pltpu.CompilerParams(vmem_limit_bytes=VMEM_LIMIT),
        cost_estimate=pl.CostEstimate(flops=flops, bytes_accessed=6_000_000, transcendentals=0),
        name="project",
    )(*[source for source, _ in pairs], *[weight for _, weight in pairs])


def finish_body(end, count, *refs):
    keeps, cores, acrosses = refs[:count], refs[count : 2 * count], refs[2 * count : 3 * count]
    out, total, sems = refs[-3:]
    copies = []
    for index in range(count):
        rows = keeps[index].shape[0]
        where = slice(end - rows, end)
        end = where.start
        part = total.at[index, :rows, :]
        value = keeps[index][...].astype(jnp.float32) + cores[index][...].astype(jnp.float32)
        part[...] = (value + acrosses[index][...].astype(jnp.float32)).astype(total.dtype)
        copies.append(pltpu.make_async_copy(part, out.at[where, :], sems.at[index]))
        copies[-1].start()
    for copy in copies:
        copy.wait()


def finish(rows, end, keeps, cores, acrosses, before=()):
    width = keeps[0].shape[1]
    count = len(keeps)
    return pl.pallas_call(
        functools.partial(finish_body, end, count),
        out_shape=rows_of(rows, width),
        in_specs=[VMEM] * (3 * count) + [HBM] * len(before),
        out_specs=HBM,
        scratch_shapes=[
            pltpu.VMEM((count, max(keep.shape[0] for keep in keeps), width), jnp.bfloat16),
            pltpu.SemaphoreType.DMA((count,)),
        ],
        input_output_aliases={3 * count: 0} if before else {},
        compiler_params=pltpu.CompilerParams(vmem_limit_bytes=VMEM_LIMIT),
        cost_estimate=COST,
        name="finish",
    )(*keeps, *cores, *acrosses, *before)


def on_device(queries, key_states, value_states, out_weight, slash_offsets, vertical_blocks):
    rows_here, per_group, head = queries.shape
    blocks = rows_here // BLOCK
    shares = (3, 3, 2)
    counts = [blocks * share // sum(shares) for share in shares]
    ctx_count = lax.axis_size("ctx")
    cfg = (slash_offsets.shape[1], ctx_count, blocks, per_group, head)

    whole = jnp.concatenate([key_states[:, 0, :], value_states[:, 0, :]], axis=1)
    one = shifted(whole, "ctx", 1)
    three = shifted(whole, "ctx", 3)
    q, w_far_send, w_far_keep, w_near_send, w_near_keep = stage(queries.transpose(1, 0, 2), out_weight, whole)
    one, q = lax.optimization_barrier((one, q))
    two = shifted(one, "ctx", 1)
    win = fill([whole, one, three], (0, 1, BAND))
    tiles = []
    if ctx_count > BAND + 1:
        start = lax.dynamic_index_in_dim(vertical_blocks[0], lax.axis_index("ctx"), 0, keepdims=False) * BLOCK
        tile = lax.dynamic_slice_in_dim(whole, start, BLOCK, 0)
        tiles.append(lax.all_gather(tile, "ctx", axis=0, tiled=True))
    info = jnp.concatenate([slash_offsets[0], vertical_blocks[0]])

    first = blocks - counts[0]
    attended, send, win = attend_early(cfg, first, counts[0], info, q, w_far_send, win, two, 2, tiles)
    sources, cores, acrosses = [attended], [swapped(send, 1)], []
    mine = None
    for count in counts[1:]:
        first -= count
        if mine is not None:
            win, mine = lax.optimization_barrier((win, mine))
            acrosses.append(swapped(mine, 2))
        attended, send, keep = attend_next(cfg, first, count, info, q, w_far_send, w_far_keep, win, sources[-1], tiles)
        mine = keep + cores[-1]
        sources.append(attended)
        cores.append(swapped(send, 1))
    acrosses.append(swapped(mine, 2))
    (keep,) = project([(sources[-1], w_far_keep)])
    mine = keep + cores[-1]
    acrosses.append(swapped(mine, 2))
    acrosses[0], mine, *sources = lax.optimization_barrier((acrosses[0], mine, *sources))
    sends = project([(source, w_near_send) for source in sources])
    keeps = project([(source, w_near_keep) for source in sources])
    cores = [swapped(send, 1) for send in sends]
    out = finish(rows_here, rows_here, keeps[:-1], cores[:-1], acrosses[:-1])
    return finish(rows_here, keeps[-1].shape[0], keeps[-1:], cores[-1:], acrosses[-1:], (out,))


def solution(mesh):
    placed = (
        P(("groups", "ctx"), "heads", None),
        P(("groups", "ctx"), "heads", None),
        P(("groups", "ctx"), "heads", None),
        P("heads", None),
        P(("groups", "heads"), None),
        P(("groups", "heads"), None),
    )
    return jax.shard_map(
        on_device,
        mesh=mesh,
        in_specs=placed,
        out_specs=P(("groups", "ctx"), "heads"),
        check_vma=False,
    )
```

```python
import functools
import math

import jax
import jax.numpy as jnp
from jax import lax
from jax.experimental import pallas as pl
from jax.experimental.pallas import tpu as pltpu
from jax.sharding import PartitionSpec as P

BLOCK = 64
BAND = 3
NEG = -1e30
VMEM_LIMIT = 12 * 1024 * 1024
COST = pl.CostEstimate(flops=1, bytes_accessed=1, transcendentals=0)
HBM = pl.BlockSpec(memory_space=pltpu.HBM)
VMEM = pl.BlockSpec(memory_space=pltpu.VMEM)
SMEM = pl.BlockSpec(memory_space=pltpu.SMEM)


def shifted(value, axis, steps):
    count = lax.axis_size(axis)
    return lax.ppermute(value, axis, [(source, source + steps) for source in range(count - steps)])


def swapped(value, flip):
    count = lax.axis_size("heads")
    return lax.ppermute(value, "heads", [(source, source ^ flip) for source in range(count)])


def block_scores(cfg, info, q_ref, win, tiles, gathered, local):
    slash, n_vert, blocks, heads_here, head = cfg
    shard = lax.axis_index("ctx")
    own = shard * blocks + local
    base = (shard - BAND) * blocks
    count = slash + n_vert
    rows = heads_here * BLOCK
    allowed = []
    for slot in range(slash):
        if slot == 0:
            source = BAND * blocks + local
            allowed.append(None)
        else:
            offset = info[slot]
            offset = jnp.where(offset == 0, info[0], offset)
            source = BAND * blocks + local - offset
            allowed.append(own - offset >= 0)
        piece = win[pl.ds(pl.multiple_of(source * BLOCK, BLOCK), BLOCK), :]
        gathered[slot * BLOCK : (slot + 1) * BLOCK, : 2 * head] = piece
    for shard_from in range(n_vert):
        slot = slash + shard_from
        column = shard_from * blocks + info[slot]
        gap = own - column
        fine = gap > 0
        for other in range(slash):
            fine = jnp.logical_and(fine, gap != info[other])
        allowed.append(fine)
        if tiles is None:
            source = jnp.where(fine, column - base, BAND * blocks + local)
            piece = win[pl.ds(pl.multiple_of(source * BLOCK, BLOCK), BLOCK), :]
        else:
            piece = tiles[shard_from * BLOCK : (shard_from + 1) * BLOCK, :]
        gathered[slot * BLOCK : (slot + 1) * BLOCK, : 2 * head] = piece
    lane = lax.broadcasted_iota(jnp.int32, (1, count * BLOCK), 1) // BLOCK
    bias = jnp.zeros((1, count * BLOCK), jnp.float32)
    for slot in range(1, count):
        bias = jnp.where(lane == slot, jnp.where(allowed[slot], 0.0, NEG), bias)
    col = lax.broadcasted_iota(jnp.int32, (BLOCK, 2 * BLOCK), 1)
    line = lax.broadcasted_iota(jnp.int32, (BLOCK, 2 * BLOCK), 0)
    near = jnp.where(jnp.logical_or(col <= line, col >= BLOCK), bias[:, : 2 * BLOCK], NEG)
    near = jnp.concatenate([near] * heads_here, axis=0)
    q = q_ref[:, local * BLOCK : (local + 1) * BLOCK, :].reshape(rows, head)
    scores = lax.dot_general(q, gathered[:, :head], (((1,), (1,)), ((), ())), preferred_element_type=jnp.float32)
    return jnp.concatenate([scores[:, : 2 * BLOCK] + near, scores[:, 2 * BLOCK :] + bias[:, 2 * BLOCK :]], axis=1)


def block_mix(cfg, scores, gathered, store):
    slash, n_vert, blocks, heads_here, head = cfg
    factor = math.log2(math.e) * head ** (-0.5)
    row_max = jnp.max(scores, axis=1, keepdims=True)
    weights = jnp.exp2((scores - row_max) * factor).astype(jnp.bfloat16)
    mixed = lax.dot_general(weights, gathered[:, head:], (((1,), (0,)), ((), ())), preferred_element_type=jnp.float32)
    result = (mixed[:, :head] / mixed[:, head:]).astype(jnp.bfloat16)
    for h in range(heads_here):
        store(h, result[h * BLOCK : (h + 1) * BLOCK])


def weight_columns(weight, block, width):
    return weight.at[:, pl.ds(pl.multiple_of(block * width, 128), width)]


def matmul(left, right, out):
    out[...] = jnp.dot(left[...], right[...], preferred_element_type=jnp.float32).astype(out.dtype)


def attend_rows(cfg, info, q_ref, win, tiles, gathered, first, attended):
    slash, n_vert, blocks, heads_here, head = cfg
    count = attended.shape[0] // BLOCK

    def scores_of(index):
        return block_scores(cfg, info, q_ref, win, tiles, gathered.at[index % gathered.shape[0]], first + index)

    scores = scores_of(0)
    for index in range(count):
        ahead = scores_of(index + 1) if index + 1 < count else None

        def store(h, value):
            attended[index * BLOCK : (index + 1) * BLOCK, h * head : (h + 1) * head] = value

        block_mix(cfg, scores, gathered.at[index % gathered.shape[0]], store)
        scores = ahead


def fill_ones(gathered, head):
    for slot in range(gathered.shape[0]):
        gathered[slot, :, 2 * head :] = jnp.ones((gathered.shape[1], head), jnp.bfloat16)


def fill_body(strides, *refs):
    win, sems = refs[-2:]
    rows = refs[0].shape[0]
    copies = []
    for index, stride in enumerate(strides):
        at = (BAND - stride) * rows
        copies.append(pltpu.make_async_copy(refs[index], win.at[at : at + rows, :], sems.at[index]))
    for copy in copies:
        copy.start()
    for copy in copies:
        copy.wait()


def fill(pieces, strides):
    rows, width = pieces[0].shape
    return pl.pallas_call(
        functools.partial(fill_body, strides),
        out_shape=rows_of((BAND + 1) * rows, width),
        in_specs=[HBM] * len(pieces),
        out_specs=VMEM,
        scratch_shapes=[pltpu.SemaphoreType.DMA((len(pieces),))],
        compiler_params=pltpu.CompilerParams(vmem_limit_bytes=VMEM_LIMIT),
        cost_estimate=COST,
        name="fill",
    )(*pieces)


def early_body(cfg, first, at, info, q_ref, w_send, held, piece, *refs):
    head = cfg[-1]
    tiles = refs[0] if len(refs) > 5 else None
    attended, send, win, gathered, sem = refs[-5:]
    copy = pltpu.make_async_copy(piece, win.at[at : at + piece.shape[0], :], sem)
    copy.start()
    fill_ones(gathered, head)
    copy.wait()
    attend_rows(cfg, info, q_ref, win, tiles, gathered, first, attended)
    matmul(attended, w_send, send)


def next_body(cfg, first, info, q_ref, w_send, w_keep, win, before, *refs):
    head = cfg[-1]
    tiles = refs[0] if len(refs) > 4 else None
    attended, send, keep, gathered = refs[-4:]
    fill_ones(gathered, head)
    matmul(before, w_keep, keep)
    attend_rows(cfg, info, q_ref, win, tiles, gathered, first, attended)
    matmul(attended, w_send, send)


def rows_of(count, like):
    return jax.ShapeDtypeStruct((count, like), jnp.bfloat16)


def kernel_params(tiles, rows):
    return dict(
        compiler_params=pltpu.CompilerParams(vmem_limit_bytes=4 * VMEM_LIMIT if tiles else VMEM_LIMIT),
        cost_estimate=pl.CostEstimate(flops=8_000_000 * rows, bytes_accessed=6_000_000, transcendentals=6000 * rows),
    )


def gather_scratch(cfg):
    return pltpu.VMEM((2, (cfg[0] + cfg[1]) * BLOCK, 3 * cfg[-1]), jnp.bfloat16)


def attend_early(cfg, first, count, info, q, w_send, win, piece, stride, tiles):
    slash, n_vert, blocks, heads_here, head = cfg
    rows = count * BLOCK
    return pl.pallas_call(
        functools.partial(early_body, cfg, first, (BAND - stride) * piece.shape[0]),
        out_shape=[rows_of(rows, heads_here * head), rows_of(rows, w_send.shape[1]), rows_of(*win.shape)],
        in_specs=[SMEM] + [VMEM] * 3 + [HBM] + [VMEM] * len(tiles),
        out_specs=[VMEM] * 3,
        scratch_shapes=[gather_scratch(cfg), pltpu.SemaphoreType.DMA],
        input_output_aliases={3: 2},
        name="attend_early",
        **kernel_params(tiles, rows),
    )(info, q, w_send, win, piece, *tiles)


def attend_next(cfg, first, count, info, q, w_send, w_keep, win, before, tiles):
    slash, n_vert, blocks, heads_here, head = cfg
    rows = count * BLOCK
    width = w_send.shape[1]
    return pl.pallas_call(
        functools.partial(next_body, cfg, first),
        out_shape=[rows_of(rows, heads_here * head), rows_of(rows, width), rows_of(before.shape[0], width)],
        in_specs=[SMEM] + [VMEM] * (5 + len(tiles)),
        out_specs=[VMEM] * 3,
        scratch_shapes=[gather_scratch(cfg)],
        name="attend_next",
        **kernel_params(tiles, rows),
    )(info, q, w_send, w_keep, win, before, *tiles)


def stage_body(queries, weight, first, q, *refs):
    slots, sems = refs[:4], refs[4]
    width = slots[0].shape[1]
    place = lax.axis_index("heads")
    copies = [pltpu.make_async_copy(queries, q, sems.at[0])]
    for index, flip in enumerate((3, 2, 1, 0)):
        copies.append(pltpu.make_async_copy(weight_columns(weight, place ^ flip, width), slots[index], sems.at[1 + index]))
    for copy in copies:
        copy.start()
    for copy in copies:
        copy.wait()


def stage(q, weight, first):
    part = jax.ShapeDtypeStruct((weight.shape[0], weight.shape[1] // 4), weight.dtype)
    return pl.pallas_call(
        stage_body,
        out_shape=[jax.ShapeDtypeStruct(q.shape, q.dtype)] + [part] * 4,
        in_specs=[HBM] * 3,
        out_specs=[VMEM] * 5,
        scratch_shapes=[pltpu.SemaphoreType.DMA((5,))],
        compiler_params=pltpu.CompilerParams(vmem_limit_bytes=VMEM_LIMIT),
        cost_estimate=COST,
        name="stage",
    )(q, weight, first)


def project_body(count, *refs):
    sources, weights, outs = refs[:count], refs[count:-count], refs[-count:]
    for source, weight, out in zip(sources, weights, outs):
        matmul(source, weight, out)


def project(pairs):
    count = len(pairs)
    flops = sum(2 * source.shape[0] * weight.shape[0] * weight.shape[1] for source, weight in pairs)
    return pl.pallas_call(
        functools.partial(project_body, count),
        out_shape=[rows_of(source.shape[0], weight.shape[1]) for source, weight in pairs],
        in_specs=[VMEM] * (2 * count),
        out_specs=[VMEM] * count,
        compiler_params=pltpu.CompilerParams(vmem_limit_bytes=VMEM_LIMIT),
        cost_estimate=pl.CostEstimate(flops=flops, bytes_accessed=6_000_000, transcendentals=0),
        name="project",
    )(*[source for source, _ in pairs], *[weight for _, weight in pairs])


def finish_body(end, count, *refs):
    keeps, cores, acrosses = refs[:count], refs[count : 2 * count], refs[2 * count : 3 * count]
    out, total, sems = refs[-3:]
    copies = []
    for index in range(count):
        rows = keeps[index].shape[0]
        where = slice(end - rows, end)
        end = where.start
        part = total.at[index, :rows, :]
        value = keeps[index][...].astype(jnp.float32) + cores[index][...].astype(jnp.float32)
        part[...] = (value + acrosses[index][...].astype(jnp.float32)).astype(total.dtype)
        copies.append(pltpu.make_async_copy(part, out.at[where, :], sems.at[index]))
        copies[-1].start()
    for copy in copies:
        copy.wait()


def finish(rows, end, keeps, cores, acrosses, before=()):
    width = keeps[0].shape[1]
    count = len(keeps)
    return pl.pallas_call(
        functools.partial(finish_body, end, count),
        out_shape=rows_of(rows, width),
        in_specs=[VMEM] * (3 * count) + [HBM] * len(before),
        out_specs=HBM,
        scratch_shapes=[
            pltpu.VMEM((count, max(keep.shape[0] for keep in keeps), width), jnp.bfloat16),
            pltpu.SemaphoreType.DMA((count,)),
        ],
        input_output_aliases={3 * count: 0} if before else {},
        compiler_params=pltpu.CompilerParams(vmem_limit_bytes=VMEM_LIMIT),
        cost_estimate=COST,
        name="finish",
    )(*keeps, *cores, *acrosses, *before)


def on_device(queries, key_states, value_states, out_weight, slash_offsets, vertical_blocks):
    rows_here, per_group, head = queries.shape
    blocks = rows_here // BLOCK
    shares = (3, 3, 2)
    counts = [blocks * share // sum(shares) for share in shares]
    ctx_count = lax.axis_size("ctx")
    cfg = (slash_offsets.shape[1], ctx_count, blocks, per_group, head)

    whole = jnp.concatenate([key_states[:, 0, :], value_states[:, 0, :]], axis=1)
    one = shifted(whole, "ctx", 1)
    three = shifted(whole, "ctx", 3)
    q, w_far_send, w_far_keep, w_near_send, w_near_keep = stage(queries.transpose(1, 0, 2), out_weight, whole)
    one, q = lax.optimization_barrier((one, q))
    two = shifted(one, "ctx", 1)
    win = fill([whole, one, three], (0, 1, BAND))
    tiles = []
    if ctx_count > BAND + 1:
        start = lax.dynamic_index_in_dim(vertical_blocks[0], lax.axis_index("ctx"), 0, keepdims=False) * BLOCK
        tile = lax.dynamic_slice_in_dim(whole, start, BLOCK, 0)
        tiles.append(lax.all_gather(tile, "ctx", axis=0, tiled=True))
    info = jnp.concatenate([slash_offsets[0], vertical_blocks[0]])

    first = blocks - counts[0]
    attended, send, win = attend_early(cfg, first, counts[0], info, q, w_far_send, win, two, 2, tiles)
    sources, cores, acrosses = [attended], [swapped(send, 1)], []
    mine = None
    for count in counts[1:]:
        first -= count
        if mine is not None:
            win, mine = lax.optimization_barrier((win, mine))
            acrosses.append(swapped(mine, 2))
        attended, send, keep = attend_next(cfg, first, count, info, q, w_far_send, w_far_keep, win, sources[-1], tiles)
        mine = keep + cores[-1]
        sources.append(attended)
        cores.append(swapped(send, 1))
    acrosses.append(swapped(mine, 2))
    (keep,) = project([(sources[-1], w_far_keep)])
    mine = keep + cores[-1]
    acrosses.append(swapped(mine, 2))
    acrosses[0], mine, *sources = lax.optimization_barrier((acrosses[0], mine, *sources))
    sends = project([(source, w_near_send) for source in sources])
    keeps = project([(source, w_near_keep) for source in sources])
    cores = [swapped(send, 1) for send in sends]
    out = finish(rows_here, rows_here, keeps[:-1], cores[:-1], acrosses[:-1])
    return finish(rows_here, keeps[-1].shape[0], keeps[-1:], cores[-1:], acrosses[-1:], (out,))


def solution(mesh):
    placed = (
        P(("groups", "ctx"), "heads", None),
        P(("groups", "ctx"), "heads", None),
        P(("groups", "ctx"), "heads", None),
        P("heads", None),
        P(("groups", "heads"), None),
        P(("groups", "heads"), None),
    )
    return jax.shard_map(
        on_device,
        mesh=mesh,
        in_specs=placed,
        out_specs=P(("groups", "ctx"), "heads"),
        check_vma=False,
    )
```

```python
import functools
import math

import jax
import jax.numpy as jnp
from jax import lax
from jax.experimental import pallas as pl
from jax.experimental.pallas import tpu as pltpu
from jax.sharding import PartitionSpec as P

BLOCK = 64
BAND = 3
NEG = -1e30
VMEM_LIMIT = 12 * 1024 * 1024
COST = pl.CostEstimate(flops=1, bytes_accessed=1, transcendentals=0)
HBM = pl.BlockSpec(memory_space=pltpu.HBM)
VMEM = pl.BlockSpec(memory_space=pltpu.VMEM)
SMEM = pl.BlockSpec(memory_space=pltpu.SMEM)


def shifted(value, axis, steps):
    count = lax.axis_size(axis)
    return lax.ppermute(value, axis, [(source, source + steps) for source in range(count - steps)])


def swapped(value, flip):
    count = lax.axis_size("heads")
    return lax.ppermute(value, "heads", [(source, source ^ flip) for source in range(count)])


def block_scores(cfg, info, q_ref, win, tiles, gathered, local):
    slash, n_vert, blocks, heads_here, head = cfg
    shard = lax.axis_index("ctx")
    own = shard * blocks + local
    base = (shard - BAND) * blocks
    count = slash + n_vert
    rows = heads_here * BLOCK
    allowed = []
    for slot in range(slash):
        if slot == 0:
            source = BAND * blocks + local
            allowed.append(None)
        else:
            offset = info[slot]
            offset = jnp.where(offset == 0, info[0], offset)
            source = BAND * blocks + local - offset
            allowed.append(own - offset >= 0)
        piece = win[pl.ds(pl.multiple_of(source * BLOCK, BLOCK), BLOCK), :]
        gathered[slot * BLOCK : (slot + 1) * BLOCK, : 2 * head] = piece
    for shard_from in range(n_vert):
        slot = slash + shard_from
        column = shard_from * blocks + info[slot]
        gap = own - column
        fine = gap > 0
        for other in range(slash):
            fine = jnp.logical_and(fine, gap != info[other])
        allowed.append(fine)
        if tiles is None:
            source = jnp.where(fine, column - base, BAND * blocks + local)
            piece = win[pl.ds(pl.multiple_of(source * BLOCK, BLOCK), BLOCK), :]
        else:
            piece = tiles[shard_from * BLOCK : (shard_from + 1) * BLOCK, :]
        gathered[slot * BLOCK : (slot + 1) * BLOCK, : 2 * head] = piece
    lane = lax.broadcasted_iota(jnp.int32, (1, count * BLOCK), 1) // BLOCK
    bias = jnp.zeros((1, count * BLOCK), jnp.float32)
    for slot in range(1, count):
        bias = jnp.where(lane == slot, jnp.where(allowed[slot], 0.0, NEG), bias)
    col = lax.broadcasted_iota(jnp.int32, (BLOCK, 2 * BLOCK), 1)
    line = lax.broadcasted_iota(jnp.int32, (BLOCK, 2 * BLOCK), 0)
    near = jnp.where(jnp.logical_or(col <= line, col >= BLOCK), bias[:, : 2 * BLOCK], NEG)
    near = jnp.concatenate([near] * heads_here, axis=0)
    q = q_ref[:, local * BLOCK : (local + 1) * BLOCK, :].reshape(rows, head)
    scores = lax.dot_general(q, gathered[:, :head], (((1,), (1,)), ((), ())), preferred_element_type=jnp.float32)
    return jnp.concatenate([scores[:, : 2 * BLOCK] + near, scores[:, 2 * BLOCK :] + bias[:, 2 * BLOCK :]], axis=1)


def block_mix(cfg, scores, gathered, store):
    slash, n_vert, blocks, heads_here, head = cfg
    factor = math.log2(math.e) * head ** (-0.5)
    row_max = jnp.max(scores, axis=1, keepdims=True)
    weights = jnp.exp2((scores - row_max) * factor).astype(jnp.bfloat16)
    mixed = lax.dot_general(weights, gathered[:, head:], (((1,), (0,)), ((), ())), preferred_element_type=jnp.float32)
    result = (mixed[:, :head] / mixed[:, head:]).astype(jnp.bfloat16)
    for h in range(heads_here):
        store(h, result[h * BLOCK : (h + 1) * BLOCK])


def weight_columns(weight, block, width):
    return weight.at[:, pl.ds(pl.multiple_of(block * width, 128), width)]


def matmul(left, right, out):
    out[...] = jnp.dot(left[...], right[...], preferred_element_type=jnp.float32).astype(out.dtype)


def attend_rows(cfg, info, q_ref, win, tiles, gathered, first, attended):
    slash, n_vert, blocks, heads_here, head = cfg
    count = attended.shape[0] // BLOCK

    def scores_of(index):
        return block_scores(cfg, info, q_ref, win, tiles, gathered.at[index % gathered.shape[0]], first + index)

    scores = scores_of(0)
    for index in range(count):
        ahead = scores_of(index + 1) if index + 1 < count else None

        def store(h, value):
            attended[index * BLOCK : (index + 1) * BLOCK, h * head : (h + 1) * head] = value

        block_mix(cfg, scores, gathered.at[index % gathered.shape[0]], store)
        scores = ahead


def fill_ones(gathered, head):
    for slot in range(gathered.shape[0]):
        gathered[slot, :, 2 * head :] = jnp.ones((gathered.shape[1], head), jnp.bfloat16)


def fill_body(strides, *refs):
    win, sems = refs[-2:]
    rows = refs[0].shape[0]
    copies = []
    for index, stride in enumerate(strides):
        at = (BAND - stride) * rows
        copies.append(pltpu.make_async_copy(refs[index], win.at[at : at + rows, :], sems.at[index]))
    for copy in copies:
        copy.start()
    for copy in copies:
        copy.wait()


def fill(pieces, strides):
    rows, width = pieces[0].shape
    return pl.pallas_call(
        functools.partial(fill_body, strides),
        out_shape=rows_of((BAND + 1) * rows, width),
        in_specs=[HBM] * len(pieces),
        out_specs=VMEM,
        scratch_shapes=[pltpu.SemaphoreType.DMA((len(pieces),))],
        compiler_params=pltpu.CompilerParams(vmem_limit_bytes=VMEM_LIMIT),
        cost_estimate=COST,
        name="fill",
    )(*pieces)


def early_body(cfg, first, at, info, q_ref, w_send, held, piece, *refs):
    head = cfg[-1]
    tiles = refs[0] if len(refs) > 5 else None
    attended, send, win, gathered, sem = refs[-5:]
    copy = pltpu.make_async_copy(piece, win.at[at : at + piece.shape[0], :], sem)
    copy.start()
    fill_ones(gathered, head)
    copy.wait()
    attend_rows(cfg, info, q_ref, win, tiles, gathered, first, attended)
    matmul(attended, w_send, send)


def next_body(cfg, first, info, q_ref, w_send, w_keep, win, before, *refs):
    head = cfg[-1]
    tiles = refs[0] if len(refs) > 4 else None
    attended, send, keep, gathered = refs[-4:]
    fill_ones(gathered, head)
    matmul(before, w_keep, keep)
    attend_rows(cfg, info, q_ref, win, tiles, gathered, first, attended)
    matmul(attended, w_send, send)


def rows_of(count, like):
    return jax.ShapeDtypeStruct((count, like), jnp.bfloat16)


def kernel_params(tiles, rows):
    return dict(
        compiler_params=pltpu.CompilerParams(vmem_limit_bytes=4 * VMEM_LIMIT if tiles else VMEM_LIMIT),
        cost_estimate=pl.CostEstimate(flops=8_000_000 * rows, bytes_accessed=6_000_000, transcendentals=6000 * rows),
    )


def gather_scratch(cfg):
    return pltpu.VMEM((2, (cfg[0] + cfg[1]) * BLOCK, 3 * cfg[-1]), jnp.bfloat16)


def attend_early(cfg, first, count, info, q, w_send, win, piece, stride, tiles):
    slash, n_vert, blocks, heads_here, head = cfg
    rows = count * BLOCK
    return pl.pallas_call(
        functools.partial(early_body, cfg, first, (BAND - stride) * piece.shape[0]),
        out_shape=[rows_of(rows, heads_here * head), rows_of(rows, w_send.shape[1]), rows_of(*win.shape)],
        in_specs=[SMEM] + [VMEM] * 3 + [HBM] + [VMEM] * len(tiles),
        out_specs=[VMEM] * 3,
        scratch_shapes=[gather_scratch(cfg), pltpu.SemaphoreType.DMA],
        input_output_aliases={3: 2},
        name="attend_early",
        **kernel_params(tiles, rows),
    )(info, q, w_send, win, piece, *tiles)


def attend_next(cfg, first, count, info, q, w_send, w_keep, win, before, tiles):
    slash, n_vert, blocks, heads_here, head = cfg
    rows = count * BLOCK
    width = w_send.shape[1]
    return pl.pallas_call(
        functools.partial(next_body, cfg, first),
        out_shape=[rows_of(rows, heads_here * head), rows_of(rows, width), rows_of(before.shape[0], width)],
        in_specs=[SMEM] + [VMEM] * (5 + len(tiles)),
        out_specs=[VMEM] * 3,
        scratch_shapes=[gather_scratch(cfg)],
        name="attend_next",
        **kernel_params(tiles, rows),
    )(info, q, w_send, w_keep, win, before, *tiles)


def stage_body(queries, weight, first, q, *refs):
    slots, sems = refs[:4], refs[4]
    width = slots[0].shape[1]
    place = lax.axis_index("heads")
    copies = [pltpu.make_async_copy(queries, q, sems.at[0])]
    for index, flip in enumerate((3, 2, 1, 0)):
        copies.append(pltpu.make_async_copy(weight_columns(weight, place ^ flip, width), slots[index], sems.at[1 + index]))
    for copy in copies:
        copy.start()
    for copy in copies:
        copy.wait()


def stage(q, weight, first):
    part = jax.ShapeDtypeStruct((weight.shape[0], weight.shape[1] // 4), weight.dtype)
    return pl.pallas_call(
        stage_body,
        out_shape=[jax.ShapeDtypeStruct(q.shape, q.dtype)] + [part] * 4,
        in_specs=[HBM] * 3,
        out_specs=[VMEM] * 5,
        scratch_shapes=[pltpu.SemaphoreType.DMA((5,))],
        compiler_params=pltpu.CompilerParams(vmem_limit_bytes=VMEM_LIMIT),
        cost_estimate=COST,
        name="stage",
    )(q, weight, first)


def project_body(count, *refs):
    sources, weights, outs = refs[:count], refs[count:-count], refs[-count:]
    for source, weight, out in zip(sources, weights, outs):
        matmul(source, weight, out)


def project(pairs):
    count = len(pairs)
    flops = sum(2 * source.shape[0] * weight.shape[0] * weight.shape[1] for source, weight in pairs)
    return pl.pallas_call(
        functools.partial(project_body, count),
        out_shape=[rows_of(source.shape[0], weight.shape[1]) for source, weight in pairs],
        in_specs=[VMEM] * (2 * count),
        out_specs=[VMEM] * count,
        compiler_params=pltpu.CompilerParams(vmem_limit_bytes=VMEM_LIMIT),
        cost_estimate=pl.CostEstimate(flops=flops, bytes_accessed=6_000_000, transcendentals=0),
        name="project",
    )(*[source for source, _ in pairs], *[weight for _, weight in pairs])


def finish_body(end, count, *refs):
    keeps, acrosses, cores = refs[:count], refs[count : 2 * count], refs[2 * count : 3 * count]
    out, total, sems = refs[-3:]
    copies = []
    for index in range(count):
        rows = keeps[index].shape[0]
        where = slice(end - rows, end)
        end = where.start
        part = total.at[index, :rows, :]
        value = keeps[index][...].astype(jnp.float32) + cores[index][...].astype(jnp.float32)
        part[...] = (value + acrosses[index][...].astype(jnp.float32)).astype(total.dtype)
        copies.append(pltpu.make_async_copy(part, out.at[where, :], sems.at[index]))
        copies[-1].start()
    for copy in copies:
        copy.wait()


def finish(rows, end, keeps, cores, acrosses, before=()):
    width = keeps[0].shape[1]
    count = len(keeps)
    return pl.pallas_call(
        functools.partial(finish_body, end, count),
        out_shape=rows_of(rows, width),
        in_specs=[VMEM] * (3 * count) + [HBM] * len(before),
        out_specs=HBM,
        scratch_shapes=[
            pltpu.VMEM((count, max(keep.shape[0] for keep in keeps), width), jnp.bfloat16),
            pltpu.SemaphoreType.DMA((count,)),
        ],
        input_output_aliases={3 * count: 0} if before else {},
        compiler_params=pltpu.CompilerParams(vmem_limit_bytes=VMEM_LIMIT),
        cost_estimate=COST,
        name="finish",
    )(*keeps, *acrosses, *cores, *before)


def on_device(queries, key_states, value_states, out_weight, slash_offsets, vertical_blocks):
    rows_here, per_group, head = queries.shape
    blocks = rows_here // BLOCK
    shares = (3, 3, 2)
    counts = [blocks * share // sum(shares) for share in shares]
    ctx_count = lax.axis_size("ctx")
    cfg = (slash_offsets.shape[1], ctx_count, blocks, per_group, head)

    whole = jnp.concatenate([key_states[:, 0, :], value_states[:, 0, :]], axis=1)
    one = shifted(whole, "ctx", 1)
    three = shifted(whole, "ctx", 3)
    q, w_far_send, w_far_keep, w_near_send, w_near_keep = stage(queries.transpose(1, 0, 2), out_weight, whole)
    one, q = lax.optimization_barrier((one, q))
    two = shifted(one, "ctx", 1)
    win = fill([whole, one, three], (0, 1, BAND))
    tiles = []
    if ctx_count > BAND + 1:
        start = lax.dynamic_index_in_dim(vertical_blocks[0], lax.axis_index("ctx"), 0, keepdims=False) * BLOCK
        tile = lax.dynamic_slice_in_dim(whole, start, BLOCK, 0)
        tiles.append(lax.all_gather(tile, "ctx", axis=0, tiled=True))
    info = jnp.concatenate([slash_offsets[0], vertical_blocks[0]])

    first = blocks - counts[0]
    attended, send, win = attend_early(cfg, first, counts[0], info, q, w_far_send, win, two, 2, tiles)
    sources, cores, acrosses = [attended], [swapped(send, 1)], []
    mine = None
    for count in counts[1:]:
        first -= count
        if mine is not None:
            win, mine = lax.optimization_barrier((win, mine))
            acrosses.append(swapped(mine, 2))
        attended, send, keep = attend_next(cfg, first, count, info, q, w_far_send, w_far_keep, win, sources[-1], tiles)
        mine = keep + cores[-1]
        mine, send = lax.optimization_barrier((mine, send))
        sources.append(attended)
        cores.append(swapped(send, 1))
    acrosses.append(swapped(mine, 2))
    (keep,) = project([(sources[-1], w_far_keep)])
    mine = keep + cores[-1]
    acrosses.append(swapped(mine, 2))
    acrosses[0], mine, *sources = lax.optimization_barrier((acrosses[0], mine, *sources))
    sends = project([(source, w_near_send) for source in sources])
    keeps = project([(source, w_near_keep) for source in sources])
    cores = [swapped(send, 1) for send in sends]
    out = finish(rows_here, rows_here, keeps[:-1], cores[:-1], acrosses[:-1])
    return finish(rows_here, keeps[-1].shape[0], keeps[-1:], cores[-1:], acrosses[-1:], (out,))


def solution(mesh):
    placed = (
        P(("groups", "ctx"), "heads", None),
        P(("groups", "ctx"), "heads", None),
        P(("groups", "ctx"), "heads", None),
        P("heads", None),
        P(("groups", "heads"), None),
        P(("groups", "heads"), None),
    )
    return jax.shard_map(
        on_device,
        mesh=mesh,
        in_specs=placed,
        out_specs=P(("groups", "ctx"), "heads"),
        check_vma=False,
    )
```
